512 devices in a mesh: gx: 32 (over z, core), gy: 16 (over x, y).
Axes of the slice: x: 4, y: 4, z: 16, core: 2. Of those that a mesh axis runs over, the one named last changes fastest.
Arguments:
- right_side: float32 [3, 512, 2048], P(None, 'gx', 'gy'), may hold values from -40 to 40
- stiffness: float32 [33, 3, 3, 512, 2048], P(None, None, None, 'gx', 'gy'), may hold values from -0.1 to 15, as said below
- factor: float32 [17, 3, 3, 512, 2048], P(None, None, None, 'gx', 'gy'), may hold values from -0.05 to 0.35, as said below
- intact: int32 [32, 512, 2048], P(None, 'gx', 'gy'), may hold values 0 or 1
Outputs:
- solution_field: float32 [3, 512, 2048], P(None, 'gx', 'gy')
- residual: float32 [3, 512, 2048], P(None, 'gx', 'gy')
The draws below stay inside these ranges and needn't reach their ends.
Inputs may be any that keep to these rules, and one draw needn't show every extreme that they name: `stiffness`: in the block for offset 16 the diagonal entries lie between 10 and 15; every other entry of every block lies within -0.1 to 0.1. `factor`: in the block for offset 16 the diagonal entries lie between 0.25 and 0.35 and its other entries within -0.02 to 0.02; the entries of the other blocks lie within -0.05 to 0.05.
All inputs are finite; a program needn't handle non-finite values. No bound on the sum of `intact` on one device may be relied on, other than what follows from the above.
Results may differ from the reference program's by a relative error of at most 0.0065.
Values sent between devices are 32-bit elements; how exact they have to be, the bound alone decides.
No kernel may reach another device: no remote copies, remote signals or barrier semaphores. Data moves between devices by JAX's collectives and lax.ppermute only.
A program may use at most 128 MiB of HBM per device.

```python
import jax
import jax.numpy as jnp
from jax import lax

NZ = 4
ITERS = 2
BONDS = 33
LOWER = 17
NX = 512
NY = 512


def draw_stiffness(key, part):
    key = jax.random.fold_in(key, 11)
    key_off = jax.random.fold_in(key, 1)
    key_diag = jax.random.fold_in(key, 2)
    shape = (BONDS, 3, 3, NX, NY * NZ)
    others = jax.random.uniform(key_off, shape, jnp.float32, -0.1, 0.1)
    diag = jax.random.uniform(key_diag, (3, NX, NY * NZ), jnp.float32, 10.0, 15.0)
    eye = jnp.eye(3, dtype=jnp.float32)[:, :, None, None]
    centre = others[16] * (1.0 - eye) + eye * diag[:, None]
    return jnp.concatenate([others[:16], centre[None], others[17:]], axis=0)


def draw_factor(key, part):
    key = jax.random.fold_in(key, 23)
    key_off = jax.random.fold_in(key, 1)
    key_diag = jax.random.fold_in(key, 2)
    key_inner = jax.random.fold_in(key, 3)
    shape = (LOWER, 3, 3, NX, NY * NZ)
    others = jax.random.uniform(key_off, shape, jnp.float32, -0.05, 0.05)
    diag = jax.random.uniform(key_diag, (3, NX, NY * NZ), jnp.float32, 0.25, 0.35)
    inner = jax.random.uniform(key_inner, (3, 3, NX, NY * NZ), jnp.float32, -0.02, 0.02)
    eye = jnp.eye(3, dtype=jnp.float32)[:, :, None, None]
    centre = inner * (1.0 - eye) + eye * diag[:, None]
    return jnp.concatenate([others[:16], centre[None]], axis=0)


def with_ends(entries, stream_key, low, high):
    shape = entries.shape
    spot = [jax.random.randint(jax.random.fold_in(stream_key, axis), (), 0, shape[axis]) for axis in range(len(shape))]
    entries = entries.at[tuple(spot)].set(low)
    longest = shape.index(max(shape))
    spot[longest] = (spot[longest] + 1) % shape[longest]
    return entries.at[tuple(spot)].set(high)


def levels(key, shape, pieces, low, largest):
    def one(position, parts):
        steps = jax.random.uniform(jax.random.fold_in(jax.random.fold_in(key, 6), position), (parts,), jnp.float32, low / len(pieces), largest / len(pieces))
        return jnp.repeat(jnp.exp(steps), shape[position] // parts).reshape((-1,) + (1,) * (len(shape) - position - 1))

    level = one(*pieces[0])
    for cut in pieces[1:]:
        level = level * one(*cut)
    return level


def scatter_about(own_key, shape, width, limit, shards=(), kind=jnp.bfloat16):
    loudness = levels(own_key, shape, shards, -0.22, 0.18) if shards else 1.0
    entries = jax.random.normal(own_key, shape, jnp.float32) * width * loudness
    return jnp.minimum(jnp.maximum(entries, -limit), limit).astype(kind)


def setup_inputs(seed: int = 0) -> dict:
    streams_of = jax.random.split(jax.random.key(seed), 5)
    right_side = scatter_about(streams_of[0], (3, NX, NY * NZ), 8.0, 40.0, ((1, 32), (2, 16)), jnp.float32)
    stiffness = draw_stiffness(jax.random.fold_in(streams_of[4], 71), 0)
    factor = draw_factor(jax.random.fold_in(streams_of[4], 71), 0)
    intact = with_ends((jax.random.randint(streams_of[3], (BONDS - 1, NX, NY * NZ), 0, 10) < 9).astype(jnp.int32), jax.random.fold_in(streams_of[3], 1), 0, 1)
    return {"right_side": right_side, "stiffness": stiffness, "factor": factor, "intact": intact}


def bond_offsets():
    return [(a, b, c) for a in range(-2, 3) for b in range(-2, 3) for c in range(-2, 3) if a * a + b * b + c * c <= 4]


def forward(blocks, extended, shift, weights, offsets):
    rows = extended.shape[1] - 2 * shift
    cols = extended.shape[2] - 2 * shift * NZ
    zpos = lax.iota(jnp.int32, cols) % NZ
    total = jnp.zeros((3, rows, cols), jnp.float32)
    for index, (dx, dy, dz) in enumerate(offsets):
        start_y = (shift + dy) * NZ + dz
        piece = extended[:, shift + dx:shift + dx + rows, start_y:start_y + cols]
        valid = ((zpos + dz >= 0) & (zpos + dz < NZ)).astype(jnp.float32)
        scale = valid if weights is None else valid * weights[index]
        total = total + jnp.sum(blocks[index] * (piece * scale)[None], axis=1)
    return total


def backward(blocks_ext, extended, margin, offsets):
    rows = extended.shape[1] - 2 * margin
    cols = extended.shape[2] - 2 * margin * NZ
    zpos = lax.iota(jnp.int32, cols) % NZ
    total = jnp.zeros((3, rows, cols), jnp.float32)
    for index, (dx, dy, dz) in enumerate(offsets):
        start_x = margin - dx
        start_y = (margin - dy) * NZ - dz
        block = blocks_ext[index, :, :, start_x:start_x + rows, start_y:start_y + cols]
        piece = extended[:, start_x:start_x + rows, start_y:start_y + cols]
        valid = ((zpos - dz >= 0) & (zpos - dz < NZ)).astype(jnp.float32)
        total = total + jnp.sum(block * (piece * valid)[:, None], axis=0)
    return total


def pad_field(field, depth):
    return jnp.pad(field, ((0, 0), (depth, depth), (depth * NZ, depth * NZ)))


def reference(right_side, stiffness, factor, intact):
    offsets = bond_offsets()
    lower = offsets[:17]
    mask = intact.astype(jnp.float32)
    weights = jnp.concatenate([mask[:16], jnp.ones_like(mask[:1]), mask[16:]], axis=0)
    factor_ext = jnp.pad(factor, ((0, 0), (0, 0), (0, 0), (2, 2), (2 * NZ, 2 * NZ)))

    def operate(field):
        return forward(stiffness, pad_field(field, 2), 2, weights, offsets)

    def precondition(field):
        image = forward(factor, pad_field(field, 2), 2, None, lower)
        return backward(factor_ext, pad_field(image, 2), 2, lower)

    solution_field = jnp.zeros_like(right_side)
    residual = right_side
    zvec = precondition(residual)
    direction = zvec
    rho = jnp.sum(residual * zvec)
    for step in range(ITERS):
        image = operate(direction)
        alpha = rho / jnp.sum(direction * image)
        solution_field = solution_field + alpha * direction
        residual = residual - alpha * image
        if step + 1 < ITERS:
            zvec = precondition(residual)
            rho_next = jnp.sum(residual * zvec)
            direction = zvec + (rho_next / rho) * direction
            rho = rho_next
    return solution_field, residual
```

```python
import jax
import jax.numpy as jnp
from jax import lax
from jax.experimental import pallas as pl
from jax.experimental.pallas import tpu as pltpu
from jax.sharding import PartitionSpec as P

NZ = 4
ROWS = 16
LANES = 128
LOWER = 17
PLANES = LOWER * 9
GROUPS = (PLANES + 7) // 8
OWN_TILES = (PLANES + 1) // 2 + 2
CENTRE = 0.8
VMEM_LIMIT = 24 * 1024 * 1024


def bond_offsets():
    return [
        (a, b, c)
        for a in range(-2, 3)
        for b in range(-2, 3)
        for c in range(-2, 3)
        if a * a + b * b + c * c <= 4
    ]


OFFSETS = bond_offsets()


def iota(rows, axis):
    return lax.broadcasted_iota(jnp.int32, (rows, LANES), axis)


def entry(p):
    return (p // 9, (p // 3) % 3, p % 3)


def pack_lanes(planes, width):
    shift = width.bit_length() - 1
    slots = LANES // width
    slot = iota(ROWS, 1) >> shift
    to_left = jnp.zeros((ROWS, LANES), jnp.float32)
    to_right = to_left
    for k, plane in enumerate(planes):
        rolled = pltpu.roll(plane, k * width, 1) if k else plane
        to_left = jnp.where(slot == k, rolled, to_left)
        to_right = jnp.where(slot == (k - 1) % slots, rolled, to_right)
    return to_left, to_right


def unpack_lanes(right, left, width, count):
    shift = width.bit_length() - 1
    even = ((iota(right.shape[0], 1) >> shift) & 1) == 0
    mixed = (jnp.where(even, right, left), jnp.where(even, left, right))
    return [pltpu.roll(mixed[k & 1], LANES - k * width, 1) if k else mixed[0] for k in range(count)]


def pack_rows(first, second):
    upper = iota(8, 0) < 4
    down = jnp.where(upper, first[:8], pltpu.roll(second[:8], 4, 0))
    up = jnp.where(upper, pltpu.roll(second[8:], 4, 0), first[8:])
    return down, up


def unpack_rows(down, up):
    upper = iota(8, 0) < 4
    return jnp.where(upper, down, up), pltpu.roll(jnp.where(upper, up, down), 4, 0)


def pack_inputs(factor, field, to_left, to_right, down, up):
    for g in range(GROUPS):
        planes = [factor[entry(p)] for p in range(8 * g, min(8 * g + 8, PLANES))]
        to_left[g], to_right[g] = pack_lanes(planes, 16)
    to_left[GROUPS], to_right[GROUPS] = pack_lanes([field[k] for k in range(3)], 32)
    for m in range(OWN_TILES - 2):
        first = factor[entry(2 * m)]
        second = factor[entry(min(2 * m + 1, PLANES - 1))]
        down[m], up[m] = pack_rows(first, second)
    down[OWN_TILES - 2], up[OWN_TILES - 2] = pack_rows(field[0], field[1])
    down[OWN_TILES - 1], up[OWN_TILES - 1] = pack_rows(field[2], field[2])


def pack_corners(right, left, down, up):
    for g in range(GROUPS + 1):
        down[g], up[g] = pack_rows(right[g], left[g])


def pack_field(field, right, left, down, up):
    down[0], up[0] = pack_rows(field[0], field[1])
    down[1], up[1] = pack_rows(field[2], field[2])
    down[2], up[2] = pack_rows(right[0], left[0])


def unpack_factor(right, left, own_down, own_up, corner_down, corner_up, edge, halo):
    for m in range(OWN_TILES - 2):
        first, second = unpack_rows(own_down[m], own_up[m])
        edge[2 * m] = first
        if 2 * m + 1 < PLANES:
            edge[2 * m + 1] = second
    for g in range(GROUPS):
        edge_right, edge_left = unpack_rows(corner_down[g], corner_up[g])
        right_all = jnp.concatenate([right[g], edge_right], axis=0)
        left_all = jnp.concatenate([left[g], edge_left], axis=0)
        count = min(8, PLANES - 8 * g)
        for k, plane in enumerate(unpack_lanes(right_all, left_all, 16, count)):
            halo[8 * g + k] = plane


def put(wide, component, tile, values):
    column = pl.ds(tile * LANES, LANES)
    wide[component, 0:8, column] = values[16:24]
    wide[component, 8:32, column] = values
    wide[component, 32:40, column] = values[0:8]


def get(wide, component, tile, shift, rows):
    return wide[component, 8 + shift : 8 + shift + rows, tile * LANES : (tile + 1) * LANES]


def shifted(near, far, by):
    if by == 0:
        return near
    lane = iota(near.shape[0], 1)
    amount = (-by) % LANES
    inside = lane < LANES - by if by > 0 else lane >= -by
    return jnp.where(inside, pltpu.roll(near, amount, 1), pltpu.roll(far, amount, 1))


def layer_ok(rows, dz):
    z = (iota(rows, 1) & (NZ - 1)) + dz
    return (z >= 0) & (z < NZ)


def clipped(values, dz):
    return values if dz == 0 else jnp.where(layer_ok(values.shape[0], dz), values, 0.0)


def by_dx(offsets):
    found = {}
    for index, (dx, dy, dz) in enumerate(offsets):
        found.setdefault(dx, []).append((index, dy, dz))
    return found


def mask_edge(values, edge_out):
    return jnp.concatenate([values[:16], jnp.where(edge_out, 0.0, values[16:24])], axis=0)


def coefficient(factor, edge, halo, plane, tile):
    if tile:
        return halo[plane]
    return jnp.concatenate([factor[entry(plane)], edge[plane]], axis=0)


def apply_factor(factor, edge, halo, wide, edge_out):
    total = [[jnp.zeros((24, LANES), jnp.float32) for _ in range(2)] for _ in range(3)]
    for dx, members in by_dx(OFFSETS[:LOWER]).items():
        base = [[get(wide, j, t, dx, 24) for t in range(2)] for j in range(3)]
        for index, dy, dz in members:
            by = dy * NZ + dz
            for j in range(3):
                for t in range(2):
                    piece = clipped(shifted(base[j][t], base[j][1 - t], by), dz)
                    for i in range(3):
                        total[i][t] += coefficient(factor, edge, halo, 9 * index + 3 * i + j, t) * piece
    return [[mask_edge(total[i][t], edge_out) for t in range(2)] for i in range(3)]


def apply_transpose(factor, edge, halo, image, wide, edge_out, side_out):
    clips = {dz: [[clipped(image[j][t], dz) for t in range(2)] for j in range(3)] for dz in range(-2, 2)}
    final = [[jnp.zeros((24, LANES), jnp.float32) for _ in range(2)] for _ in range(3)]
    for dx, members in sorted(by_dx(OFFSETS[:LOWER]).items()):
        total = [[jnp.zeros((24, LANES), jnp.float32) for _ in range(2)] for _ in range(3)]
        for index, dy, dz in members:
            by = -(dy * NZ + dz)
            for i in range(3):
                parts = []
                for t in range(2):
                    part = coefficient(factor, edge, halo, 9 * index + i, t) * clips[dz][0][t]
                    for j in range(1, 3):
                        part += coefficient(factor, edge, halo, 9 * index + 3 * j + i, t) * clips[dz][j][t]
                    parts.append(part)
                for t in range(2):
                    total[i][t] += shifted(parts[t], parts[1 - t], by)
        if dx:
            for i in range(3):
                for t in range(2):
                    put(wide, i, t, total[i][t])
            total = [[get(wide, i, t, -dx, 24) for t in range(2)] for i in range(3)]
        final = [[final[i][t] + total[i][t] for t in range(2)] for i in range(3)]
    out = []
    for i in range(3):
        row = []
        for t in range(2):
            values = mask_edge(final[i][t], edge_out)
            row.append(jnp.where(side_out, 0.0, values) if t else values)
        out.append(row)
    return out


def apply_operator(stiffness, intact, wide):
    total = [jnp.zeros((ROWS, LANES), jnp.float32) for _ in range(3)]
    for dx, members in by_dx(OFFSETS).items():
        base = [[get(wide, j, t, dx, ROWS) for t in range(2)] for j in range(3)]
        for index, dy, dz in members:
            by = dy * NZ + dz
            weight = None
            if index != 16:
                weight = clipped(intact[index if index < 16 else index - 1].astype(jnp.float32), dz)
            for j in range(3):
                piece = shifted(base[j][0], base[j][1], by)
                if weight is not None:
                    piece = piece * weight
                for i in range(3):
                    total[i] += stiffness[index, i, j] * piece
    return total


def outside(ends):
    sub = iota(8, 0)
    edge_out = ((sub < 4) & (ends[1] == 1)) | ((sub >= 4) & (ends[0] == 1))
    lane = iota(24, 1)
    side_out = ((lane < LANES // 2) & (ends[3] == 1)) | ((lane >= LANES // 2) & (ends[2] == 1))
    return edge_out, side_out


def chain(ends, factor, stiffness, intact, field, pieces, edge, halo, wide):
    edge_out, side_out = outside(ends)
    (down_a, up_a), (down_b, up_b), (down_c, up_c), right, left = pieces
    edges = [*unpack_rows(down_a, up_a), unpack_rows(down_b, up_b)[0]]
    edge_right, edge_left = unpack_rows(down_c, up_c)
    sides = unpack_lanes(
        jnp.concatenate([right, edge_right], axis=0), jnp.concatenate([left, edge_left], axis=0), 32, 3
    )
    for j in range(3):
        put(wide, j, 0, mask_edge(jnp.concatenate([field[j], edges[j]], axis=0), edge_out))
        put(wide, j, 1, mask_edge(sides[j], edge_out))
    image = apply_factor(factor, edge, halo, wide, edge_out)
    zvec = apply_transpose(factor, edge, halo, image, wide, edge_out, side_out)
    for i in range(3):
        for t in range(2):
            put(wide, i, t, zvec[i][t])
    product = apply_operator(stiffness, intact, wide)
    return [image[i][0][:ROWS] for i in range(3)], [zvec[i][0][:ROWS] for i in range(3)], product


def first_half(
    ends, factor, field, stiffness, intact, right, left, own_down, own_up, corner_down, corner_up,
    g_out, z_out, w_out, to_left, to_right, edge, halo, wide,
):
    unpack_factor(right, left, own_down, own_up, corner_down, corner_up, edge, halo)
    a, b, c = OWN_TILES - 2, OWN_TILES - 1, GROUPS
    pieces = (
        (own_down[a], own_up[a]), (own_down[b], own_up[b]), (corner_down[c], corner_up[c]), right[c], left[c],
    )
    image, zvec, product = chain(ends, factor, stiffness, intact, field, pieces, edge, halo, wide)
    for i in range(3):
        g_out[i], z_out[i], w_out[i] = image[i], zvec[i], product[i]
    to_left[0], to_right[0] = pack_lanes(product, 32)


def dot(first, second):
    whole = first[0] * second[0] + first[1] * second[1] + first[2] * second[2]
    return whole[:8] + whole[8:]


def second_half(
    ends, factor, stiffness, intact, right, left, own_down, own_up, corner_down, corner_up,
    g_in, z_in, w_in, field_right, field_left, field_down, field_up,
    u_out, au_out, sums, edge, halo, wide,
):
    unpack_factor(right, left, own_down, own_up, corner_down, corner_up, edge, halo)
    pieces = tuple((field_down[k], field_up[k]) for k in range(3)) + (field_right[0], field_left[0])
    v, u, au = chain(ends, factor, stiffness, intact, w_in, pieces, edge, halo, wide)
    for i in range(3):
        u_out[i], au_out[i] = u[i], au[i]
    g, z, w = ([ref[i] for i in range(3)] for ref in (g_in, z_in, w_in))
    g1 = [g[i] - CENTRE * v[i] for i in range(3)]
    z1 = [z[i] - CENTRE * u[i] for i in range(3)]
    az1 = [w[i] - CENTRE * au[i] for i in range(3)]
    parts = [
        dot(g, g), dot(z, w), dot(g1, g1), dot(g1, v), dot(v, v), dot(z1, az1),
        dot(u, az1) + dot(z1, au), dot(u, au), dot(z1, w) + dot(z, az1), dot(u, w) + dot(z, au),
    ]
    lane = lax.broadcasted_iota(jnp.int32, (1, LANES), 1)
    row = jnp.zeros((1, LANES), jnp.float32)
    for k, part in enumerate(parts):
        value = jnp.sum(jnp.sum(part, axis=0, keepdims=True), axis=1, keepdims=True)
        row = jnp.where(lane == k, value, row)
    for k in range(sums.shape[0]):
        sums[k] = row


def finish(sums, field, z_in, w_in, u_in, au_in, x_out, r_out):
    row = sums[0]
    for k in range(1, sums.shape[0]):
        row = row + sums[k]
    lane = lax.broadcasted_iota(jnp.int32, (1, LANES), 1)
    s = [jnp.sum(jnp.where(lane == k, row, 0.0), axis=1, keepdims=True) for k in range(10)]
    alpha = s[0] / s[1]
    off = alpha - CENTRE
    rho = s[2] - 2.0 * off * s[3] + off * off * s[4]
    beta = rho / s[0]
    zaz = s[5] - off * s[6] + off * off * s[7]
    cross = s[8] - off * s[9]
    last = rho / (zaz + beta * cross + beta * beta * s[1])
    kept = alpha + last * (1.0 + beta)
    turned = last * alpha
    for i in range(3):
        x_out[i] = kept * z_in[i] - turned * u_in[i]
        r_out[i] = field[i] - (kept * w_in[i] - turned * au_in[i])


def shape(*dims):
    return jax.ShapeDtypeStruct(dims, jnp.float32)


def call(body, name, outs, scratch=(), scalars=0):
    def run(*operands):
        specs = [pl.BlockSpec(memory_space=pltpu.SMEM)] * scalars
        specs += [pl.BlockSpec(memory_space=pltpu.VMEM)] * (len(operands) - scalars)
        return pl.pallas_call(
            body,
            out_shape=outs,
            in_specs=specs,
            out_specs=[pl.BlockSpec(memory_space=pltpu.VMEM)] * len(outs),
            scratch_shapes=list(scratch),
            compiler_params=pltpu.CompilerParams(vmem_limit_bytes=VMEM_LIMIT),
            name=name,
        )(*operands)

    return run


def swap(first, second, axis, wrap):
    count = lax.axis_size(axis)
    ends = count if wrap else count - 1
    back = [((i + 1) % count, i) for i in range(ends)]
    ahead = [(i, (i + 1) % count) for i in range(ends)]
    return lax.ppermute(first, axis, back), lax.ppermute(second, axis, ahead)


def total_of(row, axis, nxt):
    got = lax.all_to_all(row, axis, 0, 0)
    if nxt is None:
        return got
    return jnp.broadcast_to(jnp.sum(got, axis=0)[None], (nxt, 1, LANES))


def local(right_side, stiffness, factor, intact):
    gx, gy = lax.axis_index("gx"), lax.axis_index("gy")
    nx, ny = lax.axis_size("gx"), lax.axis_size("gy")
    ends = jnp.stack([gx == 0, gx == nx - 1, gy == 0, gy == ny - 1]).astype(jnp.int32)
    plane = shape(3, ROWS, LANES)
    strip = shape(GROUPS + 1, ROWS, LANES)
    own = shape(OWN_TILES, 8, LANES)
    corner = shape(GROUPS + 1, 8, LANES)
    small = shape(1, ROWS, LANES)
    edges = shape(3, 8, LANES)
    scratch = (
        pltpu.VMEM((PLANES, 8, LANES), jnp.float32),
        pltpu.VMEM((PLANES, 24, LANES), jnp.float32),
        pltpu.VMEM((3, 40, 2 * LANES), jnp.float32),
    )

    to_left, to_right, down, up = call(pack_inputs, "pack_inputs", [strip, strip, own, own])(factor, right_side)
    right, left = swap(to_left, to_right, "gy", False)
    own_down, own_up = swap(down, up, "gx", True)
    down, up = call(pack_corners, "pack_corners", [corner, corner])(right, left)
    corner_down, corner_up = swap(down, up, "gx", True)
    halos = (right, left, own_down, own_up, corner_down, corner_up)

    g, z, w, to_left, to_right = call(
        first_half, "first_half", [plane, plane, plane, small, small], scratch, 1
    )(ends, factor, right_side, stiffness, intact, *halos)
    field_right, field_left = swap(to_left, to_right, "gy", False)
    down, up = call(pack_field, "pack_field", [edges, edges])(w, field_right, field_left)
    field_down, field_up = swap(down, up, "gx", True)
    u, au, sums = call(second_half, "second_half", [plane, plane, shape(ny, 1, LANES)], scratch, 1)(
        ends, factor, stiffness, intact, *halos, g, z, w, field_right, field_left, field_down, field_up
    )
    sums = total_of(total_of(sums, "gy", nx), "gx", None)
    x, r = call(finish, "finish", [plane, plane])(sums, right_side, z, w, u, au)
    return x, r


def solution(mesh):
    in_specs = (
        P(None, "gx", "gy"),
        P(None, None, None, "gx", "gy"),
        P(None, None, None, "gx", "gy"),
        P(None, "gx", "gy"),
    )
    out_specs = (P(None, "gx", "gy"), P(None, "gx", "gy"))
    return jax.shard_map(local, mesh=mesh, in_specs=in_specs, out_specs=out_specs, check_vma=False)
```

```python
import jax
import jax.numpy as jnp
from jax import lax
from jax.experimental import pallas as pl
from jax.experimental.pallas import tpu as pltpu
from jax.sharding import PartitionSpec as P

NZ = 4
ROWS = 16
LANES = 128
LOWER = 17
PLANES = LOWER * 9
GROUPS = (PLANES + 7) // 8
OWN_TILES = (PLANES + 1) // 2 + 2
CENTRE = 0.8
VMEM_LIMIT = 24 * 1024 * 1024
WIDE_LIMIT = 53477376


def bond_offsets():
    return [
        (a, b, c)
        for a in range(-2, 3)
        for b in range(-2, 3)
        for c in range(-2, 3)
        if a * a + b * b + c * c <= 4
    ]


OFFSETS = bond_offsets()


def iota(rows, axis):
    return lax.broadcasted_iota(jnp.int32, (rows, LANES), axis)


def entry(p):
    return (p // 9, (p // 3) % 3, p % 3)


def pack_lanes(planes, width):
    shift = width.bit_length() - 1
    slots = LANES // width
    slot = iota(ROWS, 1) >> shift
    to_left = jnp.zeros((ROWS, LANES), jnp.float32)
    to_right = to_left
    for k, plane in enumerate(planes):
        rolled = pltpu.roll(plane, k * width, 1) if k else plane
        to_left = jnp.where(slot == k, rolled, to_left)
        to_right = jnp.where(slot == (k - 1) % slots, rolled, to_right)
    return to_left, to_right


def unpack_lanes(right, left, width, count):
    shift = width.bit_length() - 1
    even = ((iota(right.shape[0], 1) >> shift) & 1) == 0
    mixed = (jnp.where(even, right, left), jnp.where(even, left, right))
    return [pltpu.roll(mixed[k & 1], LANES - k * width, 1) if k else mixed[0] for k in range(count)]


def pack_rows(first, second):
    upper = iota(8, 0) < 4
    down = jnp.where(upper, first[:8], pltpu.roll(second[:8], 4, 0))
    up = jnp.where(upper, pltpu.roll(second[8:], 4, 0), first[8:])
    return down, up


def unpack_rows(down, up):
    upper = iota(8, 0) < 4
    return jnp.where(upper, down, up), pltpu.roll(jnp.where(upper, up, down), 4, 0)


CHUNKS = ((0, 5), (5, 9), (9, 13), (13, LOWER))


def pack_inputs(factor_hbm, field_hbm, factor, field, to_left, to_right, down, up, sems):
    copies = [pltpu.make_async_copy(field_hbm, field, sems.at[len(CHUNKS)])]
    for k, (low, high) in enumerate(CHUNKS):
        part = pl.ds(low, high - low)
        copies.append(pltpu.make_async_copy(factor_hbm.at[part], factor.at[part], sems.at[k]))
    for copy in copies:
        copy.start()
    copies[0].wait()
    to_left[GROUPS], to_right[GROUPS] = pack_lanes([field[k] for k in range(3)], 32)
    down[OWN_TILES - 2], up[OWN_TILES - 2] = pack_rows(field[0], field[1])
    down[OWN_TILES - 1], up[OWN_TILES - 1] = pack_rows(field[2], field[2])
    group = tile = 0
    for k, (low, high) in enumerate(CHUNKS):
        copies[1 + k].wait()
        ready = 9 * high
        while group < GROUPS and min(8 * group + 8, PLANES) <= ready:
            planes = [factor[entry(p)] for p in range(8 * group, min(8 * group + 8, PLANES))]
            to_left[group], to_right[group] = pack_lanes(planes, 16)
            group += 1
        while tile < OWN_TILES - 2 and min(2 * tile + 2, PLANES) <= ready:
            down[tile], up[tile] = pack_rows(factor[entry(2 * tile)], factor[entry(min(2 * tile + 1, PLANES - 1))])
            tile += 1


def weigh(stiffness_hbm, intact_hbm, weighted, intact, sems):
    bonds = pltpu.make_async_copy(intact_hbm, intact, sems.at[0])
    blocks = pltpu.make_async_copy(stiffness_hbm, weighted, sems.at[1])
    bonds.start()
    blocks.start()
    bonds.wait()
    blocks.wait()
    for index, (_, _, dz) in enumerate(OFFSETS):
        if index != 16:
            weight = clipped(intact[index if index < 16 else index - 1].astype(jnp.float32), dz)
            for i in range(3):
                for j in range(3):
                    weighted[index, i, j] = weighted[index, i, j] * weight


def pack_corners(right, left, down, up):
    for g in range(GROUPS + 1):
        down[g], up[g] = pack_rows(right[g], left[g])


def pack_field(field, right, left, down, up):
    down[0], up[0] = pack_rows(field[0], field[1])
    down[1], up[1] = pack_rows(field[2], field[2])
    down[2], up[2] = pack_rows(right[0], left[0])


def unpack_sides(right, left, own_down, own_up, corner_down, edge, side):
    for m in range(OWN_TILES - 2):
        first, second = unpack_rows(own_down[m], own_up[m])
        edge[2 * m] = first
        if 2 * m + 1 < PLANES:
            edge[2 * m + 1] = second
    for g in range(GROUPS):
        for k, plane in enumerate(unpack_lanes(right[g], left[g], 16, min(8, PLANES - 8 * g))):
            side[8 * g + k] = plane


def unpack_corners(corner_down, corner_up, corner):
    for g in range(GROUPS):
        right, left = unpack_rows(corner_down[g], corner_up[g])
        for k, plane in enumerate(unpack_lanes(right, left, 16, min(8, PLANES - 8 * g))):
            corner[8 * g + k] = plane


def put(wide, component, tile, values):
    column = pl.ds(tile * LANES, LANES)
    wide[component, 0:8, column] = values[16:24]
    wide[component, 8:32, column] = values
    wide[component, 32:40, column] = values[0:8]


def get(wide, component, tile, shift, rows):
    return wide[component, 8 + shift : 8 + shift + rows, tile * LANES : (tile + 1) * LANES]


def shifted(near, far, by):
    if by == 0:
        return near
    lane = iota(near.shape[0], 1)
    amount = (-by) % LANES
    inside = lane < LANES - by if by > 0 else lane >= -by
    return jnp.where(inside, pltpu.roll(near, amount, 1), pltpu.roll(far, amount, 1))


def layer_ok(rows, dz):
    z = (iota(rows, 1) & (NZ - 1)) + dz
    return (z >= 0) & (z < NZ)


def clipped(values, dz):
    return values if dz == 0 else jnp.where(layer_ok(values.shape[0], dz), values, 0.0)


def by_dx(offsets):
    found = {}
    for index, (dx, dy, dz) in enumerate(offsets):
        found.setdefault(dx, []).append((index, dy, dz))
    return found


def mask_edge(values, edge_out):
    return jnp.concatenate([values[:16], jnp.where(edge_out, 0.0, values[16:24])], axis=0)


def coefficient(blocks, plane, tile):
    factor, edge, side, corner = blocks
    if tile:
        return jnp.concatenate([side[plane], corner[plane]], axis=0)
    return jnp.concatenate([factor[entry(plane)], edge[plane]], axis=0)


def apply_factor(blocks, wide, edge_out):
    total = [[jnp.zeros((24, LANES), jnp.float32) for _ in range(2)] for _ in range(3)]
    for dx, members in by_dx(OFFSETS[:LOWER]).items():
        base = [[get(wide, j, t, dx, 24) for t in range(2)] for j in range(3)]
        for index, dy, dz in members:
            by = dy * NZ + dz
            for j in range(3):
                for t in range(2):
                    piece = clipped(shifted(base[j][t], base[j][1 - t], by), dz)
                    for i in range(3):
                        total[i][t] += coefficient(blocks, 9 * index + 3 * i + j, t) * piece
    return [[mask_edge(total[i][t], edge_out) for t in range(2)] for i in range(3)]


def apply_transpose(blocks, image, wide, edge_out, side_out):
    clips = {dz: [[clipped(image[j][t], dz) for t in range(2)] for j in range(3)] for dz in range(-2, 2)}
    final = [[jnp.zeros((24, LANES), jnp.float32) for _ in range(2)] for _ in range(3)]
    for dx, members in sorted(by_dx(OFFSETS[:LOWER]).items()):
        total = [[jnp.zeros((24, LANES), jnp.float32) for _ in range(2)] for _ in range(3)]
        for index, dy, dz in members:
            by = -(dy * NZ + dz)
            for i in range(3):
                parts = []
                for t in range(2):
                    part = coefficient(blocks, 9 * index + i, t) * clips[dz][0][t]
                    for j in range(1, 3):
                        part += coefficient(blocks, 9 * index + 3 * j + i, t) * clips[dz][j][t]
                    parts.append(part)
                for t in range(2):
                    total[i][t] += shifted(parts[t], parts[1 - t], by)
        if dx:
            for i in range(3):
                for t in range(2):
                    put(wide, i, t, total[i][t])
            total = [[get(wide, i, t, -dx, 24) for t in range(2)] for i in range(3)]
        final = [[final[i][t] + total[i][t] for t in range(2)] for i in range(3)]
    out = []
    for i in range(3):
        row = []
        for t in range(2):
            values = mask_edge(final[i][t], edge_out)
            row.append(jnp.where(side_out, 0.0, values) if t else values)
        out.append(row)
    return out


def apply_operator(weighted, wide):
    total = [jnp.zeros((ROWS, LANES), jnp.float32) for _ in range(3)]
    for dx, members in by_dx(OFFSETS).items():
        base = [[get(wide, j, t, dx, ROWS) for t in range(2)] for j in range(3)]
        for index, dy, dz in members:
            for j in range(3):
                piece = shifted(base[j][0], base[j][1], dy * NZ + dz)
                for i in range(3):
                    total[i] += weighted[index, i, j] * piece
    return total


def outside(ends):
    sub = iota(8, 0)
    edge_out = ((sub < 4) & (ends[1] == 1)) | ((sub >= 4) & (ends[0] == 1))
    lane = iota(24, 1)
    side_out = ((lane < LANES // 2) & (ends[3] == 1)) | ((lane >= LANES // 2) & (ends[2] == 1))
    return edge_out, side_out


def chain(ends, blocks, weighted, field, pieces, wide):
    edge_out, side_out = outside(ends)
    (down_a, up_a), (down_b, up_b), (down_c, up_c), right, left = pieces
    edges = [*unpack_rows(down_a, up_a), unpack_rows(down_b, up_b)[0]]
    edge_right, edge_left = unpack_rows(down_c, up_c)
    sides = unpack_lanes(
        jnp.concatenate([right, edge_right], axis=0), jnp.concatenate([left, edge_left], axis=0), 32, 3
    )
    for j in range(3):
        put(wide, j, 0, mask_edge(jnp.concatenate([field[j], edges[j]], axis=0), edge_out))
        put(wide, j, 1, mask_edge(sides[j], edge_out))
    image = apply_factor(blocks, wide, edge_out)
    zvec = apply_transpose(blocks, image, wide, edge_out, side_out)
    for i in range(3):
        for t in range(2):
            put(wide, i, t, zvec[i][t])
    product = apply_operator(weighted, wide)
    return [image[i][0][:ROWS] for i in range(3)], [zvec[i][0][:ROWS] for i in range(3)], product


def first_half(
    ends, factor, edge, side, weighted, field, right, left, own_down, own_up, corner_down, corner_up,
    corner, g_out, z_out, w_out, to_left, to_right, wide,
):
    unpack_corners(corner_down, corner_up, corner)
    a, b, c = OWN_TILES - 2, OWN_TILES - 1, GROUPS
    pieces = (
        (own_down[a], own_up[a]), (own_down[b], own_up[b]), (corner_down[c], corner_up[c]), right[c], left[c],
    )
    image, zvec, product = chain(ends, (factor, edge, side, corner), weighted, field, pieces, wide)
    for i in range(3):
        g_out[i], z_out[i], w_out[i] = image[i], zvec[i], product[i]
    to_left[0], to_right[0] = pack_lanes(product, 32)


def dot(first, second):
    whole = first[0] * second[0] + first[1] * second[1] + first[2] * second[2]
    return whole[:8] + whole[8:]


def second_half(
    ends, factor, edge, side, weighted, corner, g_in, z_in, w_in, field_right, field_left, field_down, field_up,
    u_out, au_out, sums, wide,
):
    pieces = tuple((field_down[k], field_up[k]) for k in range(3)) + (field_right[0], field_left[0])
    v, u, au = chain(ends, (factor, edge, side, corner), weighted, w_in, pieces, wide)
    for i in range(3):
        u_out[i], au_out[i] = u[i], au[i]
    g, z, w = ([ref[i] for i in range(3)] for ref in (g_in, z_in, w_in))
    g1 = [g[i] - CENTRE * v[i] for i in range(3)]
    z1 = [z[i] - CENTRE * u[i] for i in range(3)]
    az1 = [w[i] - CENTRE * au[i] for i in range(3)]
    parts = [
        dot(g, g), dot(z, w), dot(g1, g1), dot(g1, v), dot(v, v), dot(z1, az1),
        dot(u, az1) + dot(z1, au), dot(u, au), dot(z1, w) + dot(z, az1), dot(u, w) + dot(z, au),
    ]
    lane = lax.broadcasted_iota(jnp.int32, (1, LANES), 1)
    row = jnp.zeros((1, LANES), jnp.float32)
    for k, part in enumerate(parts):
        value = jnp.sum(jnp.sum(part, axis=0, keepdims=True), axis=1, keepdims=True)
        row = jnp.where(lane == k, value, row)
    for k in range(sums.shape[0]):
        sums[k] = row


def finish(sums, field, z_in, w_in, u_in, au_in, x_out, r_out):
    row = sums[...]
    lane = lax.broadcasted_iota(jnp.int32, (1, LANES), 1)
    s = [jnp.sum(jnp.where(lane == k, row, 0.0), axis=1, keepdims=True) for k in range(10)]
    alpha = s[0] / s[1]
    off = alpha - CENTRE
    rho = s[2] - 2.0 * off * s[3] + off * off * s[4]
    beta = rho / s[0]
    zaz = s[5] - off * s[6] + off * off * s[7]
    cross = s[8] - off * s[9]
    last = rho / (zaz + beta * cross + beta * beta * s[1])
    kept = alpha + last * (1.0 + beta)
    turned = last * alpha
    for i in range(3):
        x_out[i] = kept * z_in[i] - turned * u_in[i]
        r_out[i] = field[i] - (kept * w_in[i] - turned * au_in[i])


def shape(*dims):
    return jax.ShapeDtypeStruct(dims, jnp.float32)


def call(body, outs, spaces, scratch=(), cost=None, limit=VMEM_LIMIT):
    return pl.pallas_call(
        body,
        out_shape=outs,
        in_specs=[pl.BlockSpec(memory_space=space) for space in spaces],
        out_specs=[pl.BlockSpec(memory_space=pltpu.VMEM)] * len(outs),
        scratch_shapes=list(scratch),
        compiler_params=pltpu.CompilerParams(vmem_limit_bytes=limit),
        cost_estimate=cost,
        name=body.__name__,
    )


def swap(first, second, axis, wrap):
    count = lax.axis_size(axis)
    ends = count if wrap else count - 1
    back = [((i + 1) % count, i) for i in range(ends)]
    ahead = [(i, (i + 1) % count) for i in range(ends)]
    return lax.ppermute(first, axis, back), lax.ppermute(second, axis, ahead)


def gathered_sum(rows, axis):
    return jnp.sum(lax.all_to_all(rows, axis, 0, 0), axis=0)


def local(right_side, stiffness, factor, intact):
    gx, gy = lax.axis_index("gx"), lax.axis_index("gy")
    nx, ny = lax.axis_size("gx"), lax.axis_size("gy")
    ends = jnp.stack([gx == 0, gx == nx - 1, gy == 0, gy == ny - 1]).astype(jnp.int32)
    plane = shape(3, ROWS, LANES)
    strip = shape(GROUPS + 1, ROWS, LANES)
    own = shape(OWN_TILES, 8, LANES)
    ends_of_strip = shape(GROUPS + 1, 8, LANES)
    small = shape(1, ROWS, LANES)
    edges = shape(3, 8, LANES)
    tiles = shape(PLANES, 8, LANES)
    wide = pltpu.VMEM((3, 40, 2 * LANES), jnp.float32)
    vmem, hbm, smem = pltpu.VMEM, pltpu.HBM, pltpu.SMEM

    factor, field, to_left, to_right, down, up = call(
        pack_inputs,
        [shape(*factor.shape), plane, strip, strip, own, own],
        [hbm] * 2,
        [pltpu.SemaphoreType.DMA((len(CHUNKS) + 1,))],
        limit=WIDE_LIMIT,
    )(factor, right_side)
    right, left = swap(to_left, to_right, "gy", False)
    own_down, own_up = swap(down, up, "gx", True)
    (weighted,) = call(
        weigh,
        [shape(*stiffness.shape)],
        [hbm] * 2,
        [pltpu.VMEM(intact.shape, jnp.int32), pltpu.SemaphoreType.DMA((2,))],
        pl.CostEstimate(flops=stiffness.size, bytes_accessed=8 * stiffness.size, transcendentals=0),
    )(stiffness, intact)
    down, up = call(pack_corners, [ends_of_strip] * 2, [vmem] * 2)(right, left)
    edge, side = call(
        unpack_sides,
        [tiles, shape(PLANES, ROWS, LANES)],
        [vmem] * 5,
        cost=pl.CostEstimate(flops=4 * factor.size, bytes_accessed=8 * factor.size, transcendentals=0),
    )(right, left, own_down, own_up, down)
    corner_down, corner_up = swap(down, up, "gx", True)

    corner, g, z, w, to_left, to_right = call(
        first_half, [tiles, plane, plane, plane, small, small], [smem] + [vmem] * 11, [wide]
    )(ends, factor, edge, side, weighted, field, right, left, own_down, own_up, corner_down, corner_up)
    field_right, field_left = swap(to_left, to_right, "gy", False)
    down, up = call(pack_field, [edges] * 2, [vmem] * 3)(w, field_right, field_left)
    field_down, field_up = swap(down, up, "gx", True)
    u, au, sums = call(second_half, [plane, plane, shape(ny, 1, LANES)], [smem] + [vmem] * 12, [wide])(
        ends, factor, edge, side, weighted, corner, g, z, w, field_right, field_left, field_down, field_up
    )
    sums = gathered_sum(sums, "gy")
    sums = gathered_sum(jnp.broadcast_to(sums[None], (nx, 1, LANES)), "gx")
    x, r = call(finish, [plane] * 2, [vmem] * 6)(sums, field, z, w, u, au)
    return x, r


def solution(mesh):
    in_specs = (
        P(None, "gx", "gy"),
        P(None, None, None, "gx", "gy"),
        P(None, None, None, "gx", "gy"),
        P(None, "gx", "gy"),
    )
    out_specs = (P(None, "gx", "gy"), P(None, "gx", "gy"))
    return jax.shard_map(local, mesh=mesh, in_specs=in_specs, out_specs=out_specs, check_vma=False)
```

```python
import jax
import jax.numpy as jnp
from jax import lax
from jax.experimental import pallas as pl
from jax.experimental.pallas import tpu as pltpu
from jax.sharding import PartitionSpec as P

NZ = 4
ROWS = 16
LANES = 128
LOWER = 17
PLANES = LOWER * 9
GROUPS = (PLANES + 7) // 8
OWN_TILES = (PLANES + 1) // 2 + 2
CENTRE = 0.8
VMEM_LIMIT = 24 * 1024 * 1024
WIDE_LIMIT = 51 * 1024 * 1024


def bond_offsets():
    return [
        (a, b, c)
        for a in range(-2, 3)
        for b in range(-2, 3)
        for c in range(-2, 3)
        if a * a + b * b + c * c <= 4
    ]


OFFSETS = bond_offsets()


def iota(rows, axis):
    return lax.broadcasted_iota(jnp.int32, (rows, LANES), axis)


def entry(p):
    return (p // 9, (p // 3) % 3, p % 3)


def pack_lanes(planes, width):
    shift = width.bit_length() - 1
    slots = LANES // width
    slot = iota(ROWS, 1) >> shift
    to_left = jnp.zeros((ROWS, LANES), jnp.float32)
    to_right = to_left
    for k, plane in enumerate(planes):
        rolled = pltpu.roll(plane, k * width, 1) if k else plane
        to_left = jnp.where(slot == k, rolled, to_left)
        to_right = jnp.where(slot == (k - 1) % slots, rolled, to_right)
    return to_left, to_right


def unpack_lanes(right, left, width, count):
    shift = width.bit_length() - 1
    even = ((iota(right.shape[0], 1) >> shift) & 1) == 0
    mixed = (jnp.where(even, right, left), jnp.where(even, left, right))
    return [pltpu.roll(mixed[k & 1], LANES - k * width, 1) if k else mixed[0] for k in range(count)]


def pack_rows(first, second):
    upper = iota(8, 0) < 4
    down = jnp.where(upper, first[:8], pltpu.roll(second[:8], 4, 0))
    up = jnp.where(upper, pltpu.roll(second[8:], 4, 0), first[8:])
    return down, up


def unpack_rows(down, up):
    upper = iota(8, 0) < 4
    return jnp.where(upper, down, up), pltpu.roll(jnp.where(upper, up, down), 4, 0)


CHUNKS = ((0, 5), (5, 9), (9, 13), (13, LOWER))


def pack_factor(factor_hbm, factor, to_left, to_right, down, up, sems):
    copies = []
    for k, (low, high) in enumerate(CHUNKS):
        part = pl.ds(low, high - low)
        copies.append(pltpu.make_async_copy(factor_hbm.at[part], factor.at[part], sems.at[k]))
    for copy in copies:
        copy.start()
    group = tile = 0
    for k, (low, high) in enumerate(CHUNKS):
        copies[k].wait()
        ready = 9 * high
        while group < GROUPS and min(8 * group + 8, PLANES) <= ready:
            planes = [factor[entry(p)] for p in range(8 * group, min(8 * group + 8, PLANES))]
            to_left[group], to_right[group] = pack_lanes(planes, 16)
            group += 1
        while tile < OWN_TILES - 2 and min(2 * tile + 2, PLANES) <= ready:
            down[tile], up[tile] = pack_rows(factor[entry(2 * tile)], factor[entry(min(2 * tile + 1, PLANES - 1))])
            tile += 1


def pack_right_side(field, left_in, right_in, down_in, up_in, kept, to_left, to_right, down, up):
    kept[...] = field[...]
    to_left[GROUPS], to_right[GROUPS] = pack_lanes([field[k] for k in range(3)], 32)
    down[OWN_TILES - 2], up[OWN_TILES - 2] = pack_rows(field[0], field[1])
    down[OWN_TILES - 1], up[OWN_TILES - 1] = pack_rows(field[2], field[2])


def weigh(stiffness_hbm, intact_hbm, weighted, intact, sems):
    bonds = pltpu.make_async_copy(intact_hbm, intact, sems.at[0])
    blocks = pltpu.make_async_copy(stiffness_hbm, weighted, sems.at[1])
    bonds.start()
    blocks.start()
    bonds.wait()
    blocks.wait()
    for index, (_, _, dz) in enumerate(OFFSETS):
        if index != 16:
            weight = clipped(intact[index if index < 16 else index - 1].astype(jnp.float32), dz)
            for i in range(3):
                for j in range(3):
                    weighted[index, i, j] = weighted[index, i, j] * weight


def pack_corners(right, left, down, up):
    for g in range(GROUPS + 1):
        down[g], up[g] = pack_rows(right[g], left[g])


def pack_field(field, right, left, down, up):
    down[0], up[0] = pack_rows(field[0], field[1])
    down[1], up[1] = pack_rows(field[2], field[2])
    down[2], up[2] = pack_rows(right[0], left[0])


def unpack_sides(right, left, own_down, own_up, corner_down, edge, side):
    for m in range(OWN_TILES - 2):
        first, second = unpack_rows(own_down[m], own_up[m])
        edge[2 * m] = first
        if 2 * m + 1 < PLANES:
            edge[2 * m + 1] = second
    for g in range(GROUPS):
        for k, plane in enumerate(unpack_lanes(right[g], left[g], 16, min(8, PLANES - 8 * g))):
            side[8 * g + k] = plane


def unpack_corners(corner_down, corner_up, corner):
    for g in range(GROUPS):
        right, left = unpack_rows(corner_down[g], corner_up[g])
        for k, plane in enumerate(unpack_lanes(right, left, 16, min(8, PLANES - 8 * g))):
            corner[8 * g + k] = plane


def put(wide, component, tile, values):
    column = pl.ds(tile * LANES, LANES)
    wide[component, 0:8, column] = values[16:24]
    wide[component, 8:32, column] = values
    wide[component, 32:40, column] = values[0:8]


def get(wide, component, tile, shift, rows):
    return wide[component, 8 + shift : 8 + shift + rows, tile * LANES : (tile + 1) * LANES]


def shifted(near, far, by):
    if by == 0:
        return near
    lane = iota(near.shape[0], 1)
    kept = lane >= by if by > 0 else lane < LANES + by
    return pltpu.roll(jnp.where(kept, near, far), (-by) % LANES, 1)


def layer_ok(rows, dz):
    z = (iota(rows, 1) & (NZ - 1)) + dz
    return (z >= 0) & (z < NZ)


def clipped(values, dz):
    return values if dz == 0 else jnp.where(layer_ok(values.shape[0], dz), values, 0.0)


def by_dx(offsets):
    found = {}
    for index, (dx, dy, dz) in enumerate(offsets):
        found.setdefault(dx, []).append((index, dy, dz))
    return found


def mask_edge(values, edge_out):
    return jnp.concatenate([values[:16], jnp.where(edge_out, 0.0, values[16:24])], axis=0)


def coefficient(blocks, plane, tile):
    factor, edge, side, corner = blocks
    if tile:
        return jnp.concatenate([side[plane], corner[plane]], axis=0)
    return jnp.concatenate([factor[entry(plane)], edge[plane]], axis=0)


def apply_factor(blocks, wide, edge_out):
    total = [[jnp.zeros((24, LANES), jnp.float32) for _ in range(2)] for _ in range(3)]
    for dx, members in by_dx(OFFSETS[:LOWER]).items():
        base = [[get(wide, j, t, dx, 24) for t in range(2)] for j in range(3)]
        for index, dy, dz in members:
            by = dy * NZ + dz
            for j in range(3):
                for t in range(2):
                    piece = clipped(shifted(base[j][t], base[j][1 - t], by), dz)
                    for i in range(3):
                        total[i][t] += coefficient(blocks, 9 * index + 3 * i + j, t) * piece
    return [[mask_edge(total[i][t], edge_out) for t in range(2)] for i in range(3)]


def apply_transpose(blocks, image, wide, edge_out, side_out):
    clips = {dz: [[clipped(image[j][t], dz) for t in range(2)] for j in range(3)] for dz in range(-2, 2)}
    final = [[jnp.zeros((24, LANES), jnp.float32) for _ in range(2)] for _ in range(3)]
    for dx, members in sorted(by_dx(OFFSETS[:LOWER]).items()):
        total = [[jnp.zeros((24, LANES), jnp.float32) for _ in range(2)] for _ in range(3)]
        for index, dy, dz in members:
            by = -(dy * NZ + dz)
            for i in range(3):
                parts = []
                for t in range(2):
                    part = coefficient(blocks, 9 * index + i, t) * clips[dz][0][t]
                    for j in range(1, 3):
                        part += coefficient(blocks, 9 * index + 3 * j + i, t) * clips[dz][j][t]
                    parts.append(part)
                for t in range(2):
                    total[i][t] += shifted(parts[t], parts[1 - t], by)
        if dx:
            for i in range(3):
                for t in range(2):
                    put(wide, i, t, total[i][t])
            total = [[get(wide, i, t, -dx, 24) for t in range(2)] for i in range(3)]
        final = [[final[i][t] + total[i][t] for t in range(2)] for i in range(3)]
    out = []
    for i in range(3):
        row = []
        for t in range(2):
            values = mask_edge(final[i][t], edge_out)
            row.append(jnp.where(side_out, 0.0, values) if t else values)
        out.append(row)
    return out


def apply_operator(weighted, wide):
    total = [jnp.zeros((ROWS, LANES), jnp.float32) for _ in range(3)]
    for dx, members in by_dx(OFFSETS).items():
        base = [[get(wide, j, t, dx, ROWS) for t in range(2)] for j in range(3)]
        for index, dy, dz in members:
            for j in range(3):
                piece = shifted(base[j][0], base[j][1], dy * NZ + dz)
                for i in range(3):
                    total[i] += weighted[index, i, j] * piece
    return total


def outside():
    ends = []
    for axis in ("gx", "gy"):
        place = lax.axis_index(axis)
        ends += [(place == 0).astype(jnp.int32), (place == lax.axis_size(axis) - 1).astype(jnp.int32)]
    sub = iota(8, 0)
    edge_out = ((sub < 4) & (ends[1] == 1)) | ((sub >= 4) & (ends[0] == 1))
    lane = iota(24, 1)
    side_out = ((lane < LANES // 2) & (ends[3] == 1)) | ((lane >= LANES // 2) & (ends[2] == 1))
    return edge_out, side_out


def chain(blocks, weighted, field, pieces, wide):
    edge_out, side_out = outside()
    (down_a, up_a), (down_b, up_b), (down_c, up_c), right, left = pieces
    edges = [*unpack_rows(down_a, up_a), unpack_rows(down_b, up_b)[0]]
    edge_right, edge_left = unpack_rows(down_c, up_c)
    sides = unpack_lanes(
        jnp.concatenate([right, edge_right], axis=0), jnp.concatenate([left, edge_left], axis=0), 32, 3
    )
    for j in range(3):
        put(wide, j, 0, mask_edge(jnp.concatenate([field[j], edges[j]], axis=0), edge_out))
        put(wide, j, 1, mask_edge(sides[j], edge_out))
    image = apply_factor(blocks, wide, edge_out)
    zvec = apply_transpose(blocks, image, wide, edge_out, side_out)
    for i in range(3):
        for t in range(2):
            put(wide, i, t, zvec[i][t])
    product = apply_operator(weighted, wide)
    return [image[i][0][:ROWS] for i in range(3)], [zvec[i][0][:ROWS] for i in range(3)], product


def first_half(
    factor, edge, side, weighted, field, right, left, own_down, own_up, corner_down, corner_up,
    corner, g_out, z_out, w_out, to_left, to_right, wide,
):
    unpack_corners(corner_down, corner_up, corner)
    a, b, c = OWN_TILES - 2, OWN_TILES - 1, GROUPS
    pieces = (
        (own_down[a], own_up[a]), (own_down[b], own_up[b]), (corner_down[c], corner_up[c]), right[c], left[c],
    )
    image, zvec, product = chain((factor, edge, side, corner), weighted, field, pieces, wide)
    for i in range(3):
        g_out[i], z_out[i], w_out[i] = image[i], zvec[i], product[i]
    to_left[0], to_right[0] = pack_lanes(product, 32)


def dot(first, second):
    whole = first[0] * second[0] + first[1] * second[1] + first[2] * second[2]
    return whole[:8] + whole[8:]


def second_half(
    factor, edge, side, weighted, corner, g_in, z_in, w_in, field_right, field_left, field_down, field_up,
    u_out, au_out, sums, wide,
):
    pieces = tuple((field_down[k], field_up[k]) for k in range(3)) + (field_right[0], field_left[0])
    v, u, au = chain((factor, edge, side, corner), weighted, w_in, pieces, wide)
    for i in range(3):
        u_out[i], au_out[i] = u[i], au[i]
    g, z, w = ([ref[i] for i in range(3)] for ref in (g_in, z_in, w_in))
    g1 = [g[i] - CENTRE * v[i] for i in range(3)]
    z1 = [z[i] - CENTRE * u[i] for i in range(3)]
    az1 = [w[i] - CENTRE * au[i] for i in range(3)]
    parts = [
        dot(g, g), dot(z, w), dot(g1, g1), dot(g1, v), dot(v, v), dot(z1, az1),
        dot(u, az1) + dot(z1, au), dot(u, au), dot(z1, w) + dot(z, az1), dot(u, w) + dot(z, au),
    ]
    lane = lax.broadcasted_iota(jnp.int32, (1, LANES), 1)
    row = jnp.zeros((1, LANES), jnp.float32)
    for k, part in enumerate(parts):
        value = jnp.sum(jnp.sum(part, axis=0, keepdims=True), axis=1, keepdims=True)
        row = jnp.where(lane == k, value, row)
    for k in range(sums.shape[0]):
        sums[k] = row


def finish(sums, field, z_in, w_in, u_in, au_in, x_out, r_out):
    row = sums[...]
    lane = lax.broadcasted_iota(jnp.int32, (1, LANES), 1)
    s = [jnp.sum(jnp.where(lane == k, row, 0.0), axis=1, keepdims=True) for k in range(10)]
    alpha = s[0] / s[1]
    off = alpha - CENTRE
    rho = s[2] - 2.0 * off * s[3] + off * off * s[4]
    beta = rho / s[0]
    zaz = s[5] - off * s[6] + off * off * s[7]
    cross = s[8] - off * s[9]
    last = rho / (zaz + beta * cross + beta * beta * s[1])
    kept = alpha + last * (1.0 + beta)
    turned = last * alpha
    for i in range(3):
        x_out[i] = kept * z_in[i] - turned * u_in[i]
        r_out[i] = field[i] - (kept * w_in[i] - turned * au_in[i])


def shape(*dims):
    return jax.ShapeDtypeStruct(dims, jnp.float32)


def call(body, outs, spaces, scratch=(), cost=None, limit=VMEM_LIMIT, aliases=None):
    return pl.pallas_call(
        body,
        out_shape=outs,
        in_specs=[pl.BlockSpec(memory_space=space) for space in spaces],
        out_specs=[pl.BlockSpec(memory_space=pltpu.VMEM)] * len(outs),
        scratch_shapes=list(scratch),
        compiler_params=pltpu.CompilerParams(vmem_limit_bytes=limit),
        cost_estimate=cost,
        input_output_aliases=aliases or {},
        name=body.__name__,
    )


def swap(first, second, axis, wrap):
    count = lax.axis_size(axis)
    ends = count if wrap else count - 1
    back = [((i + 1) % count, i) for i in range(ends)]
    ahead = [(i, (i + 1) % count) for i in range(ends)]
    return lax.ppermute(first, axis, back), lax.ppermute(second, axis, ahead)


def gathered_sum(rows, axis):
    return jnp.sum(lax.all_to_all(rows, axis, 0, 0), axis=0)


def local(right_side, stiffness, factor, intact):
    nx, ny = lax.axis_size("gx"), lax.axis_size("gy")
    plane = shape(3, ROWS, LANES)
    strip = shape(GROUPS + 1, ROWS, LANES)
    own = shape(OWN_TILES, 8, LANES)
    ends_of_strip = shape(GROUPS + 1, 8, LANES)
    small = shape(1, ROWS, LANES)
    edges = shape(3, 8, LANES)
    tiles = shape(PLANES, 8, LANES)
    wide = pltpu.VMEM((3, 40, 2 * LANES), jnp.float32)
    vmem, hbm = pltpu.VMEM, pltpu.HBM

    factor, *packs = call(
        pack_factor,
        [shape(*factor.shape), strip, strip, own, own],
        [hbm],
        [pltpu.SemaphoreType.DMA((len(CHUNKS),))],
        limit=WIDE_LIMIT,
    )(factor)
    field, to_left, to_right, down, up = call(
        pack_right_side, [plane, strip, strip, own, own], [vmem] * 5, aliases={k: k for k in range(1, 5)}
    )(right_side, *packs)
    right, left = swap(to_left, to_right, "gy", False)
    own_down, own_up = swap(down, up, "gx", True)
    (weighted,) = call(
        weigh,
        [shape(*stiffness.shape)],
        [hbm] * 2,
        [pltpu.VMEM(intact.shape, jnp.int32), pltpu.SemaphoreType.DMA((2,))],
        pl.CostEstimate(flops=stiffness.size, bytes_accessed=8 * stiffness.size, transcendentals=0),
        WIDE_LIMIT,
    )(stiffness, intact)
    down, up = call(pack_corners, [ends_of_strip] * 2, [vmem] * 2)(right, left)
    edge, side = call(
        unpack_sides,
        [tiles, shape(PLANES, ROWS, LANES)],
        [vmem] * 5,
        cost=pl.CostEstimate(flops=4 * factor.size, bytes_accessed=8 * factor.size, transcendentals=0),
    )(right, left, own_down, own_up, down)
    corner_down, corner_up = swap(down, up, "gx", True)

    corner, g, z, w, to_left, to_right = call(
        first_half, [tiles, plane, plane, plane, small, small], [vmem] * 11, [wide]
    )(factor, edge, side, weighted, field, right, left, own_down, own_up, corner_down, corner_up)
    field_right, field_left = swap(to_left, to_right, "gy", False)
    down, up = call(pack_field, [edges] * 2, [vmem] * 3)(w, field_right, field_left)
    field_down, field_up = swap(down, up, "gx", True)
    u, au, sums = call(second_half, [plane, plane, shape(ny, 1, LANES)], [vmem] * 12, [wide])(
        factor, edge, side, weighted, corner, g, z, w, field_right, field_left, field_down, field_up
    )
    sums = gathered_sum(sums, "gy")
    sums = gathered_sum(jnp.broadcast_to(sums[None], (nx, 1, LANES)), "gx")
    x, r = call(finish, [plane] * 2, [vmem] * 6)(sums, field, z, w, u, au)
    return x, r


def solution(mesh):
    in_specs = (
        P(None, "gx", "gy"),
        P(None, None, None, "gx", "gy"),
        P(None, None, None, "gx", "gy"),
        P(None, "gx", "gy"),
    )
    out_specs = (P(None, "gx", "gy"), P(None, "gx", "gy"))
    return jax.shard_map(local, mesh=mesh, in_specs=in_specs, out_specs=out_specs, check_vma=False)
```

```python
import jax
import jax.numpy as jnp
from jax import lax
from jax.experimental import pallas as pl
from jax.experimental.pallas import tpu as pltpu
from jax.sharding import PartitionSpec as P

NZ = 4
ROWS = 16
LANES = 128
LOWER = 17
PLANES = LOWER * 9
GROUPS = (PLANES + 7) // 8
OWN_TILES = (PLANES + 1) // 2 + 2
CENTRE = 0.8
VMEM_LIMIT = 24 * 1024 * 1024
WIDE_LIMIT = 51 * 1024 * 1024


def bond_offsets():
    return [
        (a, b, c)
        for a in range(-2, 3)
        for b in range(-2, 3)
        for c in range(-2, 3)
        if a * a + b * b + c * c <= 4
    ]


OFFSETS = bond_offsets()


def iota(rows, axis):
    return lax.broadcasted_iota(jnp.int32, (rows, LANES), axis)


def entry(p):
    return (p // 9, (p // 3) % 3, p % 3)


def pack_lanes(planes, width):
    shift = width.bit_length() - 1
    slots = LANES // width
    slot = iota(ROWS, 1) >> shift
    to_left = jnp.zeros((ROWS, LANES), jnp.float32)
    to_right = to_left
    for k, plane in enumerate(planes):
        rolled = pltpu.roll(plane, k * width, 1) if k else plane
        to_left = jnp.where(slot == k, rolled, to_left)
        to_right = jnp.where(slot == (k - 1) % slots, rolled, to_right)
    return to_left, to_right


def unpack_lanes(right, left, width, count):
    shift = width.bit_length() - 1
    even = ((iota(right.shape[0], 1) >> shift) & 1) == 0
    mixed = (jnp.where(even, right, left), jnp.where(even, left, right))
    return [pltpu.roll(mixed[k & 1], LANES - k * width, 1) if k else mixed[0] for k in range(count)]


def pack_rows(first, second):
    upper = iota(8, 0) < 4
    down = jnp.where(upper, first[:8], pltpu.roll(second[:8], 4, 0))
    up = jnp.where(upper, pltpu.roll(second[8:], 4, 0), first[8:])
    return down, up


def unpack_rows(down, up):
    upper = iota(8, 0) < 4
    return jnp.where(upper, down, up), pltpu.roll(jnp.where(upper, up, down), 4, 0)


CHUNKS = ((0, 5), (5, 9), (9, 13), (13, LOWER))


def pack_factor(factor_hbm, factor, to_left, to_right, down, up, sems):
    copies = []
    for k, (low, high) in enumerate(CHUNKS):
        part = pl.ds(low, high - low)
        copies.append(pltpu.make_async_copy(factor_hbm.at[part], factor.at[part], sems.at[k]))
    for copy in copies:
        copy.start()
    group = tile = 0
    for k, (low, high) in enumerate(CHUNKS):
        copies[k].wait()
        ready = 9 * high
        while group < GROUPS and min(8 * group + 8, PLANES) <= ready:
            planes = [factor[entry(p)] for p in range(8 * group, min(8 * group + 8, PLANES))]
            to_left[group], to_right[group] = pack_lanes(planes, 16)
            group += 1
        while tile < OWN_TILES - 2 and min(2 * tile + 2, PLANES) <= ready:
            down[tile], up[tile] = pack_rows(factor[entry(2 * tile)], factor[entry(min(2 * tile + 1, PLANES - 1))])
            tile += 1


def pack_right_side(field, left_in, right_in, down_in, up_in, kept, to_left, to_right, down, up):
    kept[...] = field[...]
    to_left[GROUPS], to_right[GROUPS] = pack_lanes([field[k] for k in range(3)], 32)
    down[OWN_TILES - 2], up[OWN_TILES - 2] = pack_rows(field[0], field[1])
    down[OWN_TILES - 1], up[OWN_TILES - 1] = pack_rows(field[2], field[2])


def weigh(stiffness_hbm, intact_hbm, weighted, intact, sems):
    bonds = pltpu.make_async_copy(intact_hbm, intact, sems.at[0])
    blocks = pltpu.make_async_copy(stiffness_hbm, weighted, sems.at[1])
    bonds.start()
    blocks.start()
    bonds.wait()
    blocks.wait()
    for index, (_, _, dz) in enumerate(OFFSETS):
        if index != 16:
            weight = clipped(intact[index if index < 16 else index - 1].astype(jnp.float32), dz)
            for i in range(3):
                for j in range(3):
                    weighted[index, i, j] = weighted[index, i, j] * weight


def pack_corners(right, left, weighted, down, up):
    for g in range(GROUPS + 1):
        down[g], up[g] = pack_rows(right[g], left[g])


def pack_field(field, right, left, down, up):
    down[0], up[0] = pack_rows(field[0], field[1])
    down[1], up[1] = pack_rows(field[2], field[2])
    down[2], up[2] = pack_rows(right[0], left[0])


def unpack_sides(right, left, own_down, own_up, corner_down, edge, side):
    for m in range(OWN_TILES - 2):
        first, second = unpack_rows(own_down[m], own_up[m])
        edge[2 * m] = first
        if 2 * m + 1 < PLANES:
            edge[2 * m + 1] = second
    for g in range(GROUPS):
        for k, plane in enumerate(unpack_lanes(right[g], left[g], 16, min(8, PLANES - 8 * g))):
            side[8 * g + k] = plane


def unpack_corners(corner_down, corner_up, corner):
    for g in range(GROUPS):
        right, left = unpack_rows(corner_down[g], corner_up[g])
        for k, plane in enumerate(unpack_lanes(right, left, 16, min(8, PLANES - 8 * g))):
            corner[8 * g + k] = plane


def put(wide, component, tile, values):
    column = pl.ds(tile * LANES, LANES)
    wide[component, 0:8, column] = values[16:24]
    wide[component, 8:32, column] = values
    wide[component, 32:40, column] = values[0:8]


def get(wide, component, tile, shift, rows):
    return wide[component, 8 + shift : 8 + shift + rows, tile * LANES : (tile + 1) * LANES]


def shifted(near, far, by):
    if by == 0:
        return near
    lane = iota(near.shape[0], 1)
    kept = lane >= by if by > 0 else lane < LANES + by
    return pltpu.roll(jnp.where(kept, near, far), (-by) % LANES, 1)


def layer_ok(rows, dz):
    z = (iota(rows, 1) & (NZ - 1)) + dz
    return (z >= 0) & (z < NZ)


def clipped(values, dz):
    return values if dz == 0 else jnp.where(layer_ok(values.shape[0], dz), values, 0.0)


def by_dx(offsets):
    found = {}
    for index, (dx, dy, dz) in enumerate(offsets):
        found.setdefault(dx, []).append((index, dy, dz))
    return found


def mask_edge(values, edge_out):
    return jnp.concatenate([values[:16], jnp.where(edge_out, 0.0, values[16:24])], axis=0)


def coefficient(blocks, plane, tile):
    factor, edge, side, corner = blocks
    if tile:
        return jnp.concatenate([side[plane], corner[plane]], axis=0)
    return jnp.concatenate([factor[entry(plane)], edge[plane]], axis=0)


def apply_factor(blocks, wide, edge_out):
    total = [[jnp.zeros((24, LANES), jnp.float32) for _ in range(2)] for _ in range(3)]
    for dx, members in by_dx(OFFSETS[:LOWER]).items():
        base = [[get(wide, j, t, dx, 24) for t in range(2)] for j in range(3)]
        for index, dy, dz in members:
            by = dy * NZ + dz
            for j in range(3):
                for t in range(2):
                    piece = clipped(shifted(base[j][t], base[j][1 - t], by), dz)
                    for i in range(3):
                        total[i][t] += coefficient(blocks, 9 * index + 3 * i + j, t) * piece
    return [[mask_edge(total[i][t], edge_out) for t in range(2)] for i in range(3)]


def apply_transpose(blocks, image, wide, edge_out, side_out):
    clips = {dz: [[clipped(image[j][t], dz) for t in range(2)] for j in range(3)] for dz in range(-2, 2)}
    final = [[jnp.zeros((24, LANES), jnp.float32) for _ in range(2)] for _ in range(3)]
    for dx, members in sorted(by_dx(OFFSETS[:LOWER]).items()):
        total = [[jnp.zeros((24, LANES), jnp.float32) for _ in range(2)] for _ in range(3)]
        for index, dy, dz in members:
            by = -(dy * NZ + dz)
            for i in range(3):
                parts = []
                for t in range(2):
                    part = coefficient(blocks, 9 * index + i, t) * clips[dz][0][t]
                    for j in range(1, 3):
                        part += coefficient(blocks, 9 * index + 3 * j + i, t) * clips[dz][j][t]
                    parts.append(part)
                for t in range(2):
                    total[i][t] += shifted(parts[t], parts[1 - t], by)
        if dx:
            for i in range(3):
                for t in range(2):
                    put(wide, i, t, total[i][t])
            total = [[get(wide, i, t, -dx, 24) for t in range(2)] for i in range(3)]
        final = [[final[i][t] + total[i][t] for t in range(2)] for i in range(3)]
    out = []
    for i in range(3):
        row = []
        for t in range(2):
            values = mask_edge(final[i][t], edge_out)
            row.append(jnp.where(side_out, 0.0, values) if t else values)
        out.append(row)
    return out


def apply_operator(weighted, wide):
    total = [jnp.zeros((ROWS, LANES), jnp.float32) for _ in range(3)]
    for dx, members in by_dx(OFFSETS).items():
        base = [[get(wide, j, t, dx, ROWS) for t in range(2)] for j in range(3)]
        for index, dy, dz in members:
            for j in range(3):
                piece = shifted(base[j][0], base[j][1], dy * NZ + dz)
                for i in range(3):
                    total[i] += weighted[index, i, j] * piece
    return total


def outside():
    ends = []
    for axis in ("gx", "gy"):
        place = lax.axis_index(axis)
        ends += [(place == 0).astype(jnp.int32), (place == lax.axis_size(axis) - 1).astype(jnp.int32)]
    sub = iota(8, 0)
    edge_out = ((sub < 4) & (ends[1] == 1)) | ((sub >= 4) & (ends[0] == 1))
    lane = iota(24, 1)
    side_out = ((lane < LANES // 2) & (ends[3] == 1)) | ((lane >= LANES // 2) & (ends[2] == 1))
    return edge_out, side_out


def chain(blocks, weighted, field, pieces, wide):
    edge_out, side_out = outside()
    (down_a, up_a), (down_b, up_b), (down_c, up_c), right, left = pieces
    edges = [*unpack_rows(down_a, up_a), unpack_rows(down_b, up_b)[0]]
    edge_right, edge_left = unpack_rows(down_c, up_c)
    sides = unpack_lanes(
        jnp.concatenate([right, edge_right], axis=0), jnp.concatenate([left, edge_left], axis=0), 32, 3
    )
    for j in range(3):
        put(wide, j, 0, mask_edge(jnp.concatenate([field[j], edges[j]], axis=0), edge_out))
        put(wide, j, 1, mask_edge(sides[j], edge_out))
    image = apply_factor(blocks, wide, edge_out)
    zvec = apply_transpose(blocks, image, wide, edge_out, side_out)
    for i in range(3):
        for t in range(2):
            put(wide, i, t, zvec[i][t])
    product = apply_operator(weighted, wide)
    return [image[i][0][:ROWS] for i in range(3)], [zvec[i][0][:ROWS] for i in range(3)], product


def first_half(
    factor, edge, side, weighted, field, right, left, own_down, own_up, corner_down, corner_up,
    corner, g_out, z_out, w_out, to_left, to_right, wide,
):
    unpack_corners(corner_down, corner_up, corner)
    a, b, c = OWN_TILES - 2, OWN_TILES - 1, GROUPS
    pieces = (
        (own_down[a], own_up[a]), (own_down[b], own_up[b]), (corner_down[c], corner_up[c]), right[c], left[c],
    )
    image, zvec, product = chain((factor, edge, side, corner), weighted, field, pieces, wide)
    for i in range(3):
        g_out[i], z_out[i], w_out[i] = image[i], zvec[i], product[i]
    to_left[0], to_right[0] = pack_lanes(product, 32)


def dot(first, second):
    whole = first[0] * second[0] + first[1] * second[1] + first[2] * second[2]
    return whole[:8] + whole[8:]


def second_half(
    factor, edge, side, weighted, corner, g_in, z_in, w_in, field_right, field_left, field_down, field_up,
    u_out, au_out, sums, wide,
):
    pieces = tuple((field_down[k], field_up[k]) for k in range(3)) + (field_right[0], field_left[0])
    v, u, au = chain((factor, edge, side, corner), weighted, w_in, pieces, wide)
    for i in range(3):
        u_out[i], au_out[i] = u[i], au[i]
    g, z, w = ([ref[i] for i in range(3)] for ref in (g_in, z_in, w_in))
    g1 = [g[i] - CENTRE * v[i] for i in range(3)]
    z1 = [z[i] - CENTRE * u[i] for i in range(3)]
    az1 = [w[i] - CENTRE * au[i] for i in range(3)]
    parts = [
        dot(g, g), dot(z, w), dot(g1, g1), dot(g1, v), dot(v, v), dot(z1, az1),
        dot(u, az1) + dot(z1, au), dot(u, au), dot(z1, w) + dot(z, az1), dot(u, w) + dot(z, au),
    ]
    lane = lax.broadcasted_iota(jnp.int32, (1, LANES), 1)
    row = jnp.zeros((1, LANES), jnp.float32)
    for k, part in enumerate(parts):
        value = jnp.sum(jnp.sum(part, axis=0, keepdims=True), axis=1, keepdims=True)
        row = jnp.where(lane == k, value, row)
    for k in range(sums.shape[0]):
        sums[k] = row


def finish(sums, field, z_in, w_in, u_in, au_in, x_out, r_out):
    row = sums[...]
    lane = lax.broadcasted_iota(jnp.int32, (1, LANES), 1)
    s = [jnp.sum(jnp.where(lane == k, row, 0.0), axis=1, keepdims=True) for k in range(10)]
    alpha = s[0] / s[1]
    off = alpha - CENTRE
    rho = s[2] - 2.0 * off * s[3] + off * off * s[4]
    beta = rho / s[0]
    zaz = s[5] - off * s[6] + off * off * s[7]
    cross = s[8] - off * s[9]
    last = rho / (zaz + beta * cross + beta * beta * s[1])
    kept = alpha + last * (1.0 + beta)
    turned = last * alpha
    for i in range(3):
        x_out[i] = kept * z_in[i] - turned * u_in[i]
        r_out[i] = field[i] - (kept * w_in[i] - turned * au_in[i])


def shape(*dims):
    return jax.ShapeDtypeStruct(dims, jnp.float32)


def call(body, outs, spaces, scratch=(), cost=None, limit=VMEM_LIMIT, aliases=None):
    return pl.pallas_call(
        body,
        out_shape=outs,
        in_specs=[pl.BlockSpec(memory_space=space) for space in spaces],
        out_specs=[pl.BlockSpec(memory_space=pltpu.VMEM)] * len(outs),
        scratch_shapes=list(scratch),
        compiler_params=pltpu.CompilerParams(vmem_limit_bytes=limit),
        cost_estimate=cost,
        input_output_aliases=aliases or {},
        name=body.__name__,
    )


def swap(first, second, axis, wrap):
    count = lax.axis_size(axis)
    ends = count if wrap else count - 1
    back = [((i + 1) % count, i) for i in range(ends)]
    ahead = [(i, (i + 1) % count) for i in range(ends)]
    return lax.ppermute(first, axis, back), lax.ppermute(second, axis, ahead)


def gathered_sum(rows, axis):
    return jnp.sum(lax.all_to_all(rows, axis, 0, 0), axis=0)


def local(right_side, stiffness, factor, intact):
    nx, ny = lax.axis_size("gx"), lax.axis_size("gy")
    plane = shape(3, ROWS, LANES)
    strip = shape(GROUPS + 1, ROWS, LANES)
    own = shape(OWN_TILES, 8, LANES)
    ends_of_strip = shape(GROUPS + 1, 8, LANES)
    small = shape(1, ROWS, LANES)
    edges = shape(3, 8, LANES)
    tiles = shape(PLANES, 8, LANES)
    wide = pltpu.VMEM((3, 40, 2 * LANES), jnp.float32)
    vmem, hbm = pltpu.VMEM, pltpu.HBM

    factor, *packs = call(
        pack_factor,
        [shape(*factor.shape), strip, strip, own, own],
        [hbm],
        [pltpu.SemaphoreType.DMA((len(CHUNKS),))],
        limit=WIDE_LIMIT,
    )(factor)
    field, to_left, to_right, down, up = call(
        pack_right_side, [plane, strip, strip, own, own], [vmem] * 5, aliases={k: k for k in range(1, 5)}
    )(right_side, *packs)
    right, left = swap(to_left, to_right, "gy", False)
    own_down, own_up = swap(down, up, "gx", True)
    (weighted,) = call(
        weigh,
        [shape(*stiffness.shape)],
        [hbm] * 2,
        [pltpu.VMEM(intact.shape, jnp.int32), pltpu.SemaphoreType.DMA((2,))],
        pl.CostEstimate(flops=stiffness.size, bytes_accessed=8 * stiffness.size, transcendentals=0),
        WIDE_LIMIT,
    )(stiffness, intact)
    down, up = call(pack_corners, [ends_of_strip] * 2, [vmem] * 3)(right, left, weighted)
    edge, side = call(
        unpack_sides,
        [tiles, shape(PLANES, ROWS, LANES)],
        [vmem] * 5,
        cost=pl.CostEstimate(flops=4 * factor.size, bytes_accessed=8 * factor.size, transcendentals=0),
    )(right, left, own_down, own_up, down)
    corner_down, corner_up = swap(down, up, "gx", True)

    corner, g, z, w, to_left, to_right = call(
        first_half, [tiles, plane, plane, plane, small, small], [vmem] * 11, [wide]
    )(factor, edge, side, weighted, field, right, left, own_down, own_up, corner_down, corner_up)
    field_right, field_left = swap(to_left, to_right, "gy", False)
    down, up = call(pack_field, [edges] * 2, [vmem] * 3)(w, field_right, field_left)
    field_down, field_up = swap(down, up, "gx", True)
    u, au, sums = call(second_half, [plane, plane, shape(nx, 1, LANES)], [vmem] * 12, [wide])(
        factor, edge, side, weighted, corner, g, z, w, field_right, field_left, field_down, field_up
    )
    sums = gathered_sum(sums, "gx")
    sums = gathered_sum(jnp.broadcast_to(sums[None], (ny, 1, LANES)), "gy")
    x, r = call(finish, [plane] * 2, [vmem] * 6)(sums, field, z, w, u, au)
    return x, r


def solution(mesh):
    in_specs = (
        P(None, "gx", "gy"),
        P(None, None, None, "gx", "gy"),
        P(None, None, None, "gx", "gy"),
        P(None, "gx", "gy"),
    )
    out_specs = (P(None, "gx", "gy"), P(None, "gx", "gy"))
    return jax.shard_map(local, mesh=mesh, in_specs=in_specs, out_specs=out_specs, check_vma=False)
```

```python
import jax
import jax.numpy as jnp
from jax import lax
from jax.experimental import pallas as pl
from jax.experimental.pallas import tpu as pltpu
from jax.sharding import PartitionSpec as P

NZ = 4
ROWS = 16
LANES = 128
LOWER = 17
PLANES = LOWER * 9
OWN_TILES = (PLANES + 1) // 2 + 2
CENTRE = 0.8
VMEM_LIMIT = 24 * 1024 * 1024
WIDE_LIMIT = 51 * 1024 * 1024


def bond_offsets():
    return [
        (a, b, c)
        for a in range(-2, 3)
        for b in range(-2, 3)
        for c in range(-2, 3)
        if a * a + b * b + c * c <= 4
    ]


OFFSETS = bond_offsets()


def iota(rows, axis):
    return lax.broadcasted_iota(jnp.int32, (rows, LANES), axis)


def entry(p):
    return (p // 9, (p // 3) % 3, p % 3)


def seating():
    hosts = [(p, 3 if OFFSETS[p // 9][2] > 0 else 0) for p in range(PLANES) if abs(OFFSETS[p // 9][2]) == 1]
    below = OFFSETS.index((0, 0, -2))
    wanted = [(p, layer) for p in [*range(0, 9), *range(18, 24)] for layer in range(NZ)]
    wanted += [(p, layer) for p in range(9 * below, 9 * below + 9) for layer in (2, 3)]
    riders, seats = {}, {}
    for (guest, layer), (host, free) in zip(wanted, hosts):
        riders[host] = (guest, layer, free)
        seats.setdefault(guest, []).append((host, layer, free))
    return riders, seats


RIDERS, SEATS = seating()
CARRIERS = [p for p in range(PLANES) if p not in SEATS]
GROUPS = (len(CARRIERS) + 7) // 8
assert len(CARRIERS) % 8 == 1 and sum(map(len, SEATS.values())) == len(RIDERS)


def layer_of(rows):
    return iota(rows, 1) & (NZ - 1)


def carried(factor, p):
    plane = factor[entry(p)]
    if p in RIDERS:
        guest, layer, free = RIDERS[p]
        moved = factor[entry(guest)]
        if free != layer:
            moved = pltpu.roll(moved, (free - layer) % LANES, 1)
        plane = jnp.where(layer_of(ROWS) == free, moved, plane)
    return plane


def seat_guests(store):
    rows = store.shape[1]
    for guest, seats in SEATS.items():
        plane = None
        for host, layer, free in seats:
            moved = store[host]
            if free != layer:
                moved = pltpu.roll(moved, (layer - free) % LANES, 1)
            plane = moved if plane is None else jnp.where(layer_of(rows) == layer, moved, plane)
        store[guest] = plane


def pack_lanes(planes, width, first=0):
    shift = width.bit_length() - 1
    slots = LANES // width
    slot = iota(ROWS, 1) >> shift
    to_left = jnp.zeros((ROWS, LANES), jnp.float32)
    to_right = to_left
    for k, plane in enumerate(planes, first):
        rolled = pltpu.roll(plane, k * width, 1) if k else plane
        to_left = jnp.where(slot == k, rolled, to_left)
        to_right = jnp.where(slot == (k - 1) % slots, rolled, to_right)
    return to_left, to_right


def unpack_lanes(right, left, width, count, first=0):
    shift = width.bit_length() - 1
    even = ((iota(right.shape[0], 1) >> shift) & 1) == 0
    mixed = (jnp.where(even, right, left), jnp.where(even, left, right))
    return [pltpu.roll(mixed[k & 1], LANES - k * width, 1) if k else mixed[0] for k in range(first, first + count)]


def pack_rows(first, second):
    upper = iota(8, 0) < 4
    down = jnp.where(upper, first[:8], pltpu.roll(second[:8], 4, 0))
    up = jnp.where(upper, pltpu.roll(second[8:], 4, 0), first[8:])
    return down, up


def unpack_rows(down, up):
    upper = iota(8, 0) < 4
    return jnp.where(upper, down, up), pltpu.roll(jnp.where(upper, up, down), 4, 0)


CHUNKS = ((0, 6), (6, 11), (11, LOWER))


def pack_factor(factor_hbm, factor, to_left, to_right, down, up, sems):
    copies = []
    for k, (low, high) in enumerate(CHUNKS):
        part = pl.ds(low, high - low)
        copies.append(pltpu.make_async_copy(factor_hbm.at[part], factor.at[part], sems.at[k]))
    for copy in copies:
        copy.start()
    group = tile = 0
    for k, (low, high) in enumerate(CHUNKS):
        copies[k].wait()
        ready = 9 * high
        while group < GROUPS:
            members = CARRIERS[8 * group : 8 * group + 8]
            if max([*members, *(RIDERS[p][0] for p in members if p in RIDERS)]) >= ready:
                break
            to_left[group], to_right[group] = pack_lanes([carried(factor, p) for p in members], 16)
            group += 1
        while tile < OWN_TILES - 2 and min(2 * tile + 2, PLANES) <= ready:
            down[tile], up[tile] = pack_rows(factor[entry(2 * tile)], factor[entry(min(2 * tile + 1, PLANES - 1))])
            tile += 1


def pack_right_side(field, left_in, right_in, down_in, up_in, kept, to_left, to_right, down, up):
    kept[...] = field[...]
    last, lane = GROUPS - 1, iota(ROWS, 1)
    low, high = pack_lanes([field[k] for k in range(3)], 32, 1)
    to_left[last] = jnp.where(lane < 32, left_in[last], low)
    to_right[last] = jnp.where(lane >= 96, right_in[last], high)
    down[OWN_TILES - 2], up[OWN_TILES - 2] = pack_rows(field[0], field[1])
    down[OWN_TILES - 1], up[OWN_TILES - 1] = pack_rows(field[2], field[2])


def weigh(stiffness_hbm, intact_hbm, weighted, intact, sems):
    bonds = pltpu.make_async_copy(intact_hbm, intact, sems.at[0])
    blocks = pltpu.make_async_copy(stiffness_hbm, weighted, sems.at[1])
    bonds.start()
    blocks.start()
    bonds.wait()
    blocks.wait()
    for index, (_, _, dz) in enumerate(OFFSETS):
        if index != 16:
            weight = clipped(intact[index if index < 16 else index - 1].astype(jnp.float32), dz)
            for i in range(3):
                for j in range(3):
                    weighted[index, i, j] = weighted[index, i, j] * weight


def pack_corners(right, left, weighted, down, up):
    for g in range(GROUPS):
        down[g], up[g] = pack_rows(right[g], left[g])


def pack_field(field, right, left, down, up):
    down[0], up[0] = pack_rows(field[0], field[1])
    down[1], up[1] = pack_rows(field[2], field[2])
    down[2], up[2] = pack_rows(right[0], left[0])


def unpack_sides(right, left, own_down, own_up, corner_down, edge, side):
    for m in range(OWN_TILES - 2):
        first, second = unpack_rows(own_down[m], own_up[m])
        edge[2 * m] = first
        if 2 * m + 1 < PLANES:
            edge[2 * m + 1] = second
    for g in range(GROUPS):
        members = CARRIERS[8 * g : 8 * g + 8]
        for p, plane in zip(members, unpack_lanes(right[g], left[g], 16, len(members))):
            side[p] = plane
    seat_guests(side)


def unpack_corners(corner_down, corner_up, corner):
    for g in range(GROUPS):
        right, left = unpack_rows(corner_down[g], corner_up[g])
        members = CARRIERS[8 * g : 8 * g + 8]
        for p, plane in zip(members, unpack_lanes(right, left, 16, len(members))):
            corner[p] = plane
    seat_guests(corner)


def put(wide, component, tile, values):
    column = pl.ds(tile * LANES, LANES)
    wide[component, 0:8, column] = values[16:24]
    wide[component, 8:32, column] = values
    wide[component, 32:40, column] = values[0:8]


def get(wide, component, tile, shift, rows):
    return wide[component, 8 + shift : 8 + shift + rows, tile * LANES : (tile + 1) * LANES]


def shifted(near, far, by):
    if by == 0:
        return near
    lane = iota(near.shape[0], 1)
    kept = lane >= by if by > 0 else lane < LANES + by
    return pltpu.roll(jnp.where(kept, near, far), (-by) % LANES, 1)


def layer_ok(rows, dz):
    z = (iota(rows, 1) & (NZ - 1)) + dz
    return (z >= 0) & (z < NZ)


def clipped(values, dz):
    return values if dz == 0 else jnp.where(layer_ok(values.shape[0], dz), values, 0.0)


def by_dx(offsets):
    found = {}
    for index, (dx, dy, dz) in enumerate(offsets):
        found.setdefault(dx, []).append((index, dy, dz))
    return found


def mask_edge(values, edge_out):
    return jnp.concatenate([values[:16], jnp.where(edge_out, 0.0, values[16:24])], axis=0)


def coefficient(blocks, plane, tile):
    factor, edge, side, corner = blocks
    if tile:
        return jnp.concatenate([side[plane], corner[plane]], axis=0)
    return jnp.concatenate([factor[entry(plane)], edge[plane]], axis=0)


def apply_factor(blocks, wide, edge_out):
    total = [[jnp.zeros((24, LANES), jnp.float32) for _ in range(2)] for _ in range(3)]
    for dx, members in by_dx(OFFSETS[:LOWER]).items():
        base = [[get(wide, j, t, dx, 24) for t in range(2)] for j in range(3)]
        for index, dy, dz in members:
            by = dy * NZ + dz
            for j in range(3):
                for t in range(2):
                    piece = clipped(shifted(base[j][t], base[j][1 - t], by), dz)
                    for i in range(3):
                        total[i][t] += coefficient(blocks, 9 * index + 3 * i + j, t) * piece
    return [[mask_edge(total[i][t], edge_out) for t in range(2)] for i in range(3)]


def apply_transpose(blocks, image, wide, edge_out, side_out):
    clips = {dz: [[clipped(image[j][t], dz) for t in range(2)] for j in range(3)] for dz in range(-2, 2)}
    final = [[jnp.zeros((24, LANES), jnp.float32) for _ in range(2)] for _ in range(3)]
    for dx, members in sorted(by_dx(OFFSETS[:LOWER]).items()):
        total = [[jnp.zeros((24, LANES), jnp.float32) for _ in range(2)] for _ in range(3)]
        for index, dy, dz in members:
            by = -(dy * NZ + dz)
            for i in range(3):
                parts = []
                for t in range(2):
                    part = coefficient(blocks, 9 * index + i, t) * clips[dz][0][t]
                    for j in range(1, 3):
                        part += coefficient(blocks, 9 * index + 3 * j + i, t) * clips[dz][j][t]
                    parts.append(part)
                for t in range(2):
                    total[i][t] += shifted(parts[t], parts[1 - t], by)
        if dx:
            for i in range(3):
                for t in range(2):
                    put(wide, i, t, total[i][t])
            total = [[get(wide, i, t, -dx, 24) for t in range(2)] for i in range(3)]
        final = [[final[i][t] + total[i][t] for t in range(2)] for i in range(3)]
    out = []
    for i in range(3):
        row = []
        for t in range(2):
            values = mask_edge(final[i][t], edge_out)
            row.append(jnp.where(side_out, 0.0, values) if t else values)
        out.append(row)
    return out


def apply_operator(weighted, wide):
    total = [jnp.zeros((ROWS, LANES), jnp.float32) for _ in range(3)]
    for dx, members in by_dx(OFFSETS).items():
        base = [[get(wide, j, t, dx, ROWS) for t in range(2)] for j in range(3)]
        for index, dy, dz in members:
            for j in range(3):
                piece = shifted(base[j][0], base[j][1], dy * NZ + dz)
                for i in range(3):
                    total[i] += weighted[index, i, j] * piece
    return total


def outside():
    ends = []
    for axis in ("gx", "gy"):
        place = lax.axis_index(axis)
        ends += [(place == 0).astype(jnp.int32), (place == lax.axis_size(axis) - 1).astype(jnp.int32)]
    sub = iota(8, 0)
    edge_out = ((sub < 4) & (ends[1] == 1)) | ((sub >= 4) & (ends[0] == 1))
    lane = iota(24, 1)
    side_out = ((lane < LANES // 2) & (ends[3] == 1)) | ((lane >= LANES // 2) & (ends[2] == 1))
    return edge_out, side_out


def chain(blocks, weighted, field, pieces, wide):
    edge_out, side_out = outside()
    (down_a, up_a), (down_b, up_b), (down_c, up_c), right, left = pieces
    edges = [*unpack_rows(down_a, up_a), unpack_rows(down_b, up_b)[0]]
    edge_right, edge_left = unpack_rows(down_c, up_c)
    sides = unpack_lanes(
        jnp.concatenate([right, edge_right], axis=0), jnp.concatenate([left, edge_left], axis=0), 32, 3, 1
    )
    for j in range(3):
        put(wide, j, 0, mask_edge(jnp.concatenate([field[j], edges[j]], axis=0), edge_out))
        put(wide, j, 1, mask_edge(sides[j], edge_out))
    image = apply_factor(blocks, wide, edge_out)
    zvec = apply_transpose(blocks, image, wide, edge_out, side_out)
    for i in range(3):
        for t in range(2):
            put(wide, i, t, zvec[i][t])
    product = apply_operator(weighted, wide)
    return [image[i][0][:ROWS] for i in range(3)], [zvec[i][0][:ROWS] for i in range(3)], product


def first_half(
    factor, edge, side, weighted, field, right, left, own_down, own_up, corner_down, corner_up,
    corner, g_out, z_out, w_out, to_left, to_right, wide,
):
    unpack_corners(corner_down, corner_up, corner)
    a, b, c = OWN_TILES - 2, OWN_TILES - 1, GROUPS - 1
    pieces = (
        (own_down[a], own_up[a]), (own_down[b], own_up[b]), (corner_down[c], corner_up[c]), right[c], left[c],
    )
    image, zvec, product = chain((factor, edge, side, corner), weighted, field, pieces, wide)
    for i in range(3):
        g_out[i], z_out[i], w_out[i] = image[i], zvec[i], product[i]
    to_left[0], to_right[0] = pack_lanes(product, 32, 1)


def dot(first, second):
    whole = first[0] * second[0] + first[1] * second[1] + first[2] * second[2]
    return whole[:8] + whole[8:]


def second_half(
    factor, edge, side, weighted, corner, g_in, z_in, w_in, field_right, field_left, field_down, field_up,
    u_out, au_out, sums, wide,
):
    pieces = tuple((field_down[k], field_up[k]) for k in range(3)) + (field_right[0], field_left[0])
    v, u, au = chain((factor, edge, side, corner), weighted, w_in, pieces, wide)
    for i in range(3):
        u_out[i], au_out[i] = u[i], au[i]
    g, z, w = ([ref[i] for i in range(3)] for ref in (g_in, z_in, w_in))
    g1 = [g[i] - CENTRE * v[i] for i in range(3)]
    z1 = [z[i] - CENTRE * u[i] for i in range(3)]
    az1 = [w[i] - CENTRE * au[i] for i in range(3)]
    parts = [
        dot(g, g), dot(z, w), dot(g1, g1), dot(g1, v), dot(v, v), dot(z1, az1),
        dot(u, az1) + dot(z1, au), dot(u, au), dot(z1, w) + dot(z, az1), dot(u, w) + dot(z, au),
    ]
    lane = lax.broadcasted_iota(jnp.int32, (1, LANES), 1)
    row = jnp.zeros((1, LANES), jnp.float32)
    for k, part in enumerate(parts):
        value = jnp.sum(jnp.sum(part, axis=0, keepdims=True), axis=1, keepdims=True)
        row = jnp.where(lane == k, value, row)
    for k in range(sums.shape[0]):
        sums[k] = row


def finish(sums, field, z_in, w_in, u_in, au_in, x_out, r_out):
    row = sums[...]
    lane = lax.broadcasted_iota(jnp.int32, (1, LANES), 1)
    s = [jnp.sum(jnp.where(lane == k, row, 0.0), axis=1, keepdims=True) for k in range(10)]
    alpha = s[0] / s[1]
    off = alpha - CENTRE
    rho = s[2] - 2.0 * off * s[3] + off * off * s[4]
    beta = rho / s[0]
    zaz = s[5] - off * s[6] + off * off * s[7]
    cross = s[8] - off * s[9]
    last = rho / (zaz + beta * cross + beta * beta * s[1])
    kept = alpha + last * (1.0 + beta)
    turned = last * alpha
    for i in range(3):
        x_out[i] = kept * z_in[i] - turned * u_in[i]
        r_out[i] = field[i] - (kept * w_in[i] - turned * au_in[i])


def shape(*dims):
    return jax.ShapeDtypeStruct(dims, jnp.float32)


def call(body, outs, spaces, scratch=(), cost=None, limit=VMEM_LIMIT, aliases=None):
    return pl.pallas_call(
        body,
        out_shape=outs,
        in_specs=[pl.BlockSpec(memory_space=space) for space in spaces],
        out_specs=[pl.BlockSpec(memory_space=pltpu.VMEM)] * len(outs),
        scratch_shapes=list(scratch),
        compiler_params=pltpu.CompilerParams(vmem_limit_bytes=limit),
        cost_estimate=cost,
        input_output_aliases=aliases or {},
        name=body.__name__,
    )


def swap(first, second, axis, wrap):
    count = lax.axis_size(axis)
    ends = count if wrap else count - 1
    back = [((i + 1) % count, i) for i in range(ends)]
    ahead = [(i, (i + 1) % count) for i in range(ends)]
    return lax.ppermute(first, axis, back), lax.ppermute(second, axis, ahead)


def gathered_sum(rows, axis):
    return jnp.sum(lax.all_to_all(rows, axis, 0, 0), axis=0)


def local(right_side, stiffness, factor, intact):
    nx, ny = lax.axis_size("gx"), lax.axis_size("gy")
    plane = shape(3, ROWS, LANES)
    strip = shape(GROUPS, ROWS, LANES)
    own = shape(OWN_TILES, 8, LANES)
    ends_of_strip = shape(GROUPS, 8, LANES)
    small = shape(1, ROWS, LANES)
    edges = shape(3, 8, LANES)
    tiles = shape(PLANES, 8, LANES)
    wide = pltpu.VMEM((3, 40, 2 * LANES), jnp.float32)
    vmem, hbm = pltpu.VMEM, pltpu.HBM

    factor, *packs = call(
        pack_factor,
        [shape(*factor.shape), strip, strip, own, own],
        [hbm],
        [pltpu.SemaphoreType.DMA((len(CHUNKS),))],
        limit=WIDE_LIMIT,
    )(factor)
    field, to_left, to_right, down, up = call(
        pack_right_side, [plane, strip, strip, own, own], [vmem] * 5, aliases={k: k for k in range(1, 5)}
    )(right_side, *packs)
    right, left = swap(to_left, to_right, "gy", False)
    own_down, own_up = swap(down, up, "gx", True)
    (weighted,) = call(
        weigh,
        [shape(*stiffness.shape)],
        [hbm] * 2,
        [pltpu.VMEM(intact.shape, jnp.int32), pltpu.SemaphoreType.DMA((2,))],
        pl.CostEstimate(flops=stiffness.size, bytes_accessed=8 * stiffness.size, transcendentals=0),
        WIDE_LIMIT,
    )(stiffness, intact)
    down, up = call(pack_corners, [ends_of_strip] * 2, [vmem] * 3)(right, left, weighted)
    edge, side = call(
        unpack_sides,
        [tiles, shape(PLANES, ROWS, LANES)],
        [vmem] * 5,
        cost=pl.CostEstimate(flops=4 * factor.size, bytes_accessed=8 * factor.size, transcendentals=0),
    )(right, left, own_down, own_up, down)
    corner_down, corner_up = swap(down, up, "gx", True)

    corner, g, z, w, to_left, to_right = call(
        first_half, [tiles, plane, plane, plane, small, small], [vmem] * 11, [wide]
    )(factor, edge, side, weighted, field, right, left, own_down, own_up, corner_down, corner_up)
    field_right, field_left = swap(to_left, to_right, "gy", False)
    down, up = call(pack_field, [edges] * 2, [vmem] * 3)(w, field_right, field_left)
    field_down, field_up = swap(down, up, "gx", True)
    u, au, sums = call(second_half, [plane, plane, shape(nx, 1, LANES)], [vmem] * 12, [wide])(
        factor, edge, side, weighted, corner, g, z, w, field_right, field_left, field_down, field_up
    )
    sums = gathered_sum(sums, "gx")
    sums = gathered_sum(jnp.broadcast_to(sums[None], (ny, 1, LANES)), "gy")
    x, r = call(finish, [plane] * 2, [vmem] * 6)(sums, field, z, w, u, au)
    return x, r


def solution(mesh):
    in_specs = (
        P(None, "gx", "gy"),
        P(None, None, None, "gx", "gy"),
        P(None, None, None, "gx", "gy"),
        P(None, "gx", "gy"),
    )
    out_specs = (P(None, "gx", "gy"), P(None, "gx", "gy"))
    return jax.shard_map(local, mesh=mesh, in_specs=in_specs, out_specs=out_specs, check_vma=False)
```

```python
import jax
import jax.numpy as jnp
from jax import lax
from jax.experimental import pallas as pl
from jax.experimental.pallas import tpu as pltpu
from jax.sharding import PartitionSpec as P

NZ = 4
ROWS = 16
LANES = 128
LOWER = 17
PLANES = LOWER * 9
OWN_TILES = (PLANES + 1) // 2 + 2
CENTRE = 0.8
VMEM_LIMIT = 24 * 1024 * 1024
WIDE_LIMIT = 51 * 1024 * 1024


def bond_offsets():
    return [
        (a, b, c)
        for a in range(-2, 3)
        for b in range(-2, 3)
        for c in range(-2, 3)
        if a * a + b * b + c * c <= 4
    ]


OFFSETS = bond_offsets()


def iota(rows, axis):
    return lax.broadcasted_iota(jnp.int32, (rows, LANES), axis)


def entry(p):
    return (p // 9, (p // 3) % 3, p % 3)


def seating():
    hosts = [(p, 3 if OFFSETS[p // 9][2] > 0 else 0) for p in range(PLANES) if abs(OFFSETS[p // 9][2]) == 1]
    below = OFFSETS.index((0, 0, -2))
    wanted = [(p, layer) for p in [*range(0, 9), *range(18, 24)] for layer in range(NZ)]
    wanted += [(p, layer) for p in range(9 * below, 9 * below + 9) for layer in (2, 3)]
    riders, seats = {}, {}
    for (guest, layer), (host, free) in zip(wanted, hosts):
        riders[host] = (guest, layer, free)
        seats.setdefault(guest, []).append((host, layer, free))
    return riders, seats


RIDERS, SEATS = seating()
CARRIERS = [p for p in range(PLANES) if p not in SEATS]
GROUPS = (len(CARRIERS) + 7) // 8
assert len(CARRIERS) % 8 == 1 and sum(map(len, SEATS.values())) == len(RIDERS)


def layer_of(rows):
    return iota(rows, 1) & (NZ - 1)


def carried(factor, p):
    plane = factor[entry(p)]
    if p in RIDERS:
        guest, layer, free = RIDERS[p]
        moved = factor[entry(guest)]
        if free != layer:
            moved = pltpu.roll(moved, (free - layer) % LANES, 1)
        plane = jnp.where(layer_of(ROWS) == free, moved, plane)
    return plane


def seat_guests(store):
    rows = store.shape[1]
    for guest, seats in SEATS.items():
        plane = None
        for host, layer, free in seats:
            moved = store[host]
            if free != layer:
                moved = pltpu.roll(moved, (layer - free) % LANES, 1)
            plane = moved if plane is None else jnp.where(layer_of(rows) == layer, moved, plane)
        store[guest] = plane


def pack_lanes(planes, width, first=0):
    shift = width.bit_length() - 1
    slots = LANES // width
    slot = iota(ROWS, 1) >> shift
    halves = [None, None]
    for k, plane in enumerate(planes, first):
        rolled = pltpu.roll(plane, k * width, 1) if k else plane
        held = halves[k & 1]
        if held is not None:
            rolled = jnp.where((slot == k) | (slot == (k - 1) % slots), rolled, held)
        halves[k & 1] = rolled
    even, odd = (jnp.zeros((ROWS, LANES), jnp.float32) if half is None else half for half in halves)
    is_even = (slot & 1) == 0
    return jnp.where(is_even, even, odd), jnp.where(is_even, odd, even)


def unpack_lanes(right, left, width, count, first=0):
    shift = width.bit_length() - 1
    even = ((iota(right.shape[0], 1) >> shift) & 1) == 0
    mixed = (jnp.where(even, right, left), jnp.where(even, left, right))
    return [pltpu.roll(mixed[k & 1], LANES - k * width, 1) if k else mixed[0] for k in range(first, first + count)]


def pack_rows(first, second):
    upper = iota(8, 0) < 4
    down = jnp.where(upper, first[:8], pltpu.roll(second[:8], 4, 0))
    up = jnp.where(upper, pltpu.roll(second[8:], 4, 0), first[8:])
    return down, up


def unpack_rows(down, up):
    upper = iota(8, 0) < 4
    return jnp.where(upper, down, up), pltpu.roll(jnp.where(upper, up, down), 4, 0)


CHUNKS = ((0, 6), (6, 11), (11, LOWER))


def pack_factor(factor_hbm, factor, to_left, to_right, down, up, sems):
    copies = []
    for k, (low, high) in enumerate(CHUNKS):
        part = pl.ds(low, high - low)
        copies.append(pltpu.make_async_copy(factor_hbm.at[part], factor.at[part], sems.at[k]))
    for copy in copies:
        copy.start()
    group = tile = 0
    for k, (low, high) in enumerate(CHUNKS):
        copies[k].wait()
        ready = 9 * high
        while group < GROUPS:
            members = CARRIERS[8 * group : 8 * group + 8]
            if max([*members, *(RIDERS[p][0] for p in members if p in RIDERS)]) >= ready:
                break
            to_left[group], to_right[group] = pack_lanes([carried(factor, p) for p in members], 16)
            group += 1
        while tile < OWN_TILES - 2 and min(2 * tile + 2, PLANES) <= ready:
            down[tile], up[tile] = pack_rows(factor[entry(2 * tile)], factor[entry(min(2 * tile + 1, PLANES - 1))])
            tile += 1


def pack_right_side(field, left_in, right_in, down_in, up_in, kept, to_left, to_right, down, up):
    kept[...] = field[...]
    for held, packed in ((left_in, to_left), (right_in, to_right), (down_in, down), (up_in, up)):
        packed[...] = held[...]
    last, lane = GROUPS - 1, iota(ROWS, 1)
    low, high = pack_lanes([field[k] for k in range(3)], 32, 1)
    to_left[last] = jnp.where(lane < 32, left_in[last], low)
    to_right[last] = jnp.where(lane >= 96, right_in[last], high)
    down[OWN_TILES - 2], up[OWN_TILES - 2] = pack_rows(field[0], field[1])
    down[OWN_TILES - 1], up[OWN_TILES - 1] = pack_rows(field[2], field[2])


def weigh(stiffness_hbm, intact_hbm, weighted, intact, sems):
    bonds = pltpu.make_async_copy(intact_hbm, intact, sems.at[0])
    blocks = pltpu.make_async_copy(stiffness_hbm, weighted, sems.at[1])
    bonds.start()
    blocks.start()
    bonds.wait()
    blocks.wait()
    for index, (_, _, dz) in enumerate(OFFSETS):
        if index != 16:
            weight = clipped(intact[index if index < 16 else index - 1].astype(jnp.float32), dz)
            for i in range(3):
                for j in range(3):
                    weighted[index, i, j] = weighted[index, i, j] * weight


def pack_corners(right, left, weighted, down, up):
    for g in range(GROUPS):
        down[g], up[g] = pack_rows(right[g], left[g])


def pack_field(field, right, left, down, up):
    down[0], up[0] = pack_rows(field[0], field[1])
    down[1], up[1] = pack_rows(field[2], field[2])
    down[2], up[2] = pack_rows(right[0], left[0])


def unpack_sides(right, left, own_down, own_up, corner_down, edge, side):
    for m in range(OWN_TILES - 2):
        first, second = unpack_rows(own_down[m], own_up[m])
        edge[2 * m] = first
        if 2 * m + 1 < PLANES:
            edge[2 * m + 1] = second
    for g in range(GROUPS):
        members = CARRIERS[8 * g : 8 * g + 8]
        for p, plane in zip(members, unpack_lanes(right[g], left[g], 16, len(members))):
            side[p] = plane
    seat_guests(side)


def unpack_corners(corner_down, corner_up, corner):
    for g in range(GROUPS):
        right, left = unpack_rows(corner_down[g], corner_up[g])
        members = CARRIERS[8 * g : 8 * g + 8]
        for p, plane in zip(members, unpack_lanes(right, left, 16, len(members))):
            corner[p] = plane
    seat_guests(corner)


def put(wide, component, tile, values):
    column = pl.ds(tile * LANES, LANES)
    wide[component, 0:8, column] = values[16:24]
    wide[component, 8:32, column] = values
    wide[component, 32:40, column] = values[0:8]


def get(wide, component, tile, shift, rows):
    return wide[component, 8 + shift : 8 + shift + rows, tile * LANES : (tile + 1) * LANES]


def shifted(near, far, by):
    if by == 0:
        return near
    lane = iota(near.shape[0], 1)
    kept = lane >= by if by > 0 else lane < LANES + by
    return pltpu.roll(jnp.where(kept, near, far), (-by) % LANES, 1)


def layer_ok(rows, dz):
    z = (iota(rows, 1) & (NZ - 1)) + dz
    return (z >= 0) & (z < NZ)


def clipped(values, dz):
    return values if dz == 0 else jnp.where(layer_ok(values.shape[0], dz), values, 0.0)


def by_dx(offsets):
    found = {}
    for index, (dx, dy, dz) in enumerate(offsets):
        found.setdefault(dx, []).append((index, dy, dz))
    return found


def mask_edge(values, edge_out):
    return jnp.concatenate([values[:16], jnp.where(edge_out, 0.0, values[16:24])], axis=0)


def coefficient(blocks, plane, tile):
    factor, edge, side, corner = blocks
    if tile:
        return jnp.concatenate([side[plane], corner[plane]], axis=0)
    return jnp.concatenate([factor[entry(plane)], edge[plane]], axis=0)


def apply_factor(blocks, wide, edge_out):
    total = [[jnp.zeros((24, LANES), jnp.float32) for _ in range(2)] for _ in range(3)]
    for dx, members in by_dx(OFFSETS[:LOWER]).items():
        base = [[get(wide, j, t, dx, 24) for t in range(2)] for j in range(3)]
        for index, dy, dz in members:
            by = dy * NZ + dz
            for j in range(3):
                for t in range(2):
                    piece = clipped(shifted(base[j][t], base[j][1 - t], by), dz)
                    for i in range(3):
                        total[i][t] += coefficient(blocks, 9 * index + 3 * i + j, t) * piece
    return [[mask_edge(total[i][t], edge_out) for t in range(2)] for i in range(3)]


def apply_transpose(blocks, image, wide, edge_out, side_out):
    clips = {dz: [[clipped(image[j][t], dz) for t in range(2)] for j in range(3)] for dz in range(-2, 2)}
    final = [[jnp.zeros((24, LANES), jnp.float32) for _ in range(2)] for _ in range(3)]
    for dx, members in sorted(by_dx(OFFSETS[:LOWER]).items()):
        total = [[jnp.zeros((24, LANES), jnp.float32) for _ in range(2)] for _ in range(3)]
        for index, dy, dz in members:
            by = -(dy * NZ + dz)
            for i in range(3):
                parts = []
                for t in range(2):
                    part = coefficient(blocks, 9 * index + i, t) * clips[dz][0][t]
                    for j in range(1, 3):
                        part += coefficient(blocks, 9 * index + 3 * j + i, t) * clips[dz][j][t]
                    parts.append(part)
                for t in range(2):
                    total[i][t] += shifted(parts[t], parts[1 - t], by)
        if dx:
            for i in range(3):
                for t in range(2):
                    put(wide, i, t, total[i][t])
            total = [[get(wide, i, t, -dx, 24) for t in range(2)] for i in range(3)]
        final = [[final[i][t] + total[i][t] for t in range(2)] for i in range(3)]
    out = []
    for i in range(3):
        row = []
        for t in range(2):
            values = mask_edge(final[i][t], edge_out)
            row.append(jnp.where(side_out, 0.0, values) if t else values)
        out.append(row)
    return out


def apply_operator(weighted, wide):
    total = [jnp.zeros((ROWS, LANES), jnp.float32) for _ in range(3)]
    for dx, members in by_dx(OFFSETS).items():
        base = [[get(wide, j, t, dx, ROWS) for t in range(2)] for j in range(3)]
        for index, dy, dz in members:
            for j in range(3):
                piece = shifted(base[j][0], base[j][1], dy * NZ + dz)
                for i in range(3):
                    total[i] += weighted[index, i, j] * piece
    return total


def outside():
    ends = []
    for axis in ("gx", "gy"):
        place = lax.axis_index(axis)
        ends += [(place == 0).astype(jnp.int32), (place == lax.axis_size(axis) - 1).astype(jnp.int32)]
    sub = iota(8, 0)
    edge_out = ((sub < 4) & (ends[1] == 1)) | ((sub >= 4) & (ends[0] == 1))
    lane = iota(24, 1)
    side_out = ((lane < LANES // 2) & (ends[3] == 1)) | ((lane >= LANES // 2) & (ends[2] == 1))
    return edge_out, side_out


def chain(blocks, weighted, field, pieces, wide):
    edge_out, side_out = outside()
    (down_a, up_a), (down_b, up_b), (down_c, up_c), right, left = pieces
    edges = [*unpack_rows(down_a, up_a), unpack_rows(down_b, up_b)[0]]
    edge_right, edge_left = unpack_rows(down_c, up_c)
    sides = unpack_lanes(
        jnp.concatenate([right, edge_right], axis=0), jnp.concatenate([left, edge_left], axis=0), 32, 3, 1
    )
    for j in range(3):
        put(wide, j, 0, mask_edge(jnp.concatenate([field[j], edges[j]], axis=0), edge_out))
        put(wide, j, 1, mask_edge(sides[j], edge_out))
    image = apply_factor(blocks, wide, edge_out)
    zvec = apply_transpose(blocks, image, wide, edge_out, side_out)
    for i in range(3):
        for t in range(2):
            put(wide, i, t, zvec[i][t])
    product = apply_operator(weighted, wide)
    return [image[i][0][:ROWS] for i in range(3)], [zvec[i][0][:ROWS] for i in range(3)], product


def first_half(
    factor, edge, side, weighted, field, right, left, own_down, own_up, corner_down, corner_up,
    corner, g_out, z_out, w_out, to_left, to_right, wide,
):
    unpack_corners(corner_down, corner_up, corner)
    a, b, c = OWN_TILES - 2, OWN_TILES - 1, GROUPS - 1
    pieces = (
        (own_down[a], own_up[a]), (own_down[b], own_up[b]), (corner_down[c], corner_up[c]), right[c], left[c],
    )
    image, zvec, product = chain((factor, edge, side, corner), weighted, field, pieces, wide)
    for i in range(3):
        g_out[i], z_out[i], w_out[i] = image[i], zvec[i], product[i]
    to_left[0], to_right[0] = pack_lanes(product, 32, 1)


def dot(first, second):
    whole = first[0] * second[0] + first[1] * second[1] + first[2] * second[2]
    return whole[:8] + whole[8:]


def second_half(
    factor, edge, side, weighted, corner, g_in, z_in, w_in, field_right, field_left, field_down, field_up,
    u_out, au_out, sums, wide,
):
    pieces = tuple((field_down[k], field_up[k]) for k in range(3)) + (field_right[0], field_left[0])
    v, u, au = chain((factor, edge, side, corner), weighted, w_in, pieces, wide)
    for i in range(3):
        u_out[i], au_out[i] = u[i], au[i]
    g, z, w = ([ref[i] for i in range(3)] for ref in (g_in, z_in, w_in))
    g1 = [g[i] - CENTRE * v[i] for i in range(3)]
    z1 = [z[i] - CENTRE * u[i] for i in range(3)]
    az1 = [w[i] - CENTRE * au[i] for i in range(3)]
    parts = [
        dot(g, g), dot(z, w), dot(g1, g1), dot(g1, v), dot(v, v), dot(z1, az1),
        dot(u, az1) + dot(z1, au), dot(u, au), dot(z1, w) + dot(z, az1), dot(u, w) + dot(z, au),
    ]
    lane = lax.broadcasted_iota(jnp.int32, (1, LANES), 1)
    row = jnp.zeros((1, LANES), jnp.float32)
    for k, part in enumerate(parts):
        value = jnp.sum(jnp.sum(part, axis=0, keepdims=True), axis=1, keepdims=True)
        row = jnp.where(lane == k, value, row)
    for k in range(sums.shape[0]):
        sums[k] = row


def finish(sums, field, z_in, w_in, u_in, au_in, x_out, r_out):
    row = sums[...]
    lane = lax.broadcasted_iota(jnp.int32, (1, LANES), 1)
    s = [jnp.sum(jnp.where(lane == k, row, 0.0), axis=1, keepdims=True) for k in range(10)]
    alpha = s[0] / s[1]
    off = alpha - CENTRE
    rho = s[2] - 2.0 * off * s[3] + off * off * s[4]
    beta = rho / s[0]
    zaz = s[5] - off * s[6] + off * off * s[7]
    cross = s[8] - off * s[9]
    last = rho / (zaz + beta * cross + beta * beta * s[1])
    kept = alpha + last * (1.0 + beta)
    turned = last * alpha
    for i in range(3):
        x_out[i] = kept * z_in[i] - turned * u_in[i]
        r_out[i] = field[i] - (kept * w_in[i] - turned * au_in[i])


def shape(*dims):
    return jax.ShapeDtypeStruct(dims, jnp.float32)


def call(body, outs, spaces, scratch=(), cost=None, limit=VMEM_LIMIT, aliases=None):
    return pl.pallas_call(
        body,
        out_shape=outs,
        in_specs=[pl.BlockSpec(memory_space=space) for space in spaces],
        out_specs=[pl.BlockSpec(memory_space=pltpu.VMEM)] * len(outs),
        scratch_shapes=list(scratch),
        compiler_params=pltpu.CompilerParams(vmem_limit_bytes=limit),
        cost_estimate=cost,
        input_output_aliases=aliases or {},
        name=body.__name__,
    )


def swap(first, second, axis, wrap):
    count = lax.axis_size(axis)
    ends = count if wrap else count - 1
    back = [((i + 1) % count, i) for i in range(ends)]
    ahead = [(i, (i + 1) % count) for i in range(ends)]
    return lax.ppermute(first, axis, back), lax.ppermute(second, axis, ahead)


def gathered_sum(rows, axis):
    return jnp.sum(lax.all_to_all(rows, axis, 0, 0), axis=0)


def local(right_side, stiffness, factor, intact):
    nx, ny = lax.axis_size("gx"), lax.axis_size("gy")
    plane = shape(3, ROWS, LANES)
    strip = shape(GROUPS, ROWS, LANES)
    own = shape(OWN_TILES, 8, LANES)
    ends_of_strip = shape(GROUPS, 8, LANES)
    small = shape(1, ROWS, LANES)
    edges = shape(3, 8, LANES)
    tiles = shape(PLANES, 8, LANES)
    wide = pltpu.VMEM((3, 40, 2 * LANES), jnp.float32)
    vmem, hbm = pltpu.VMEM, pltpu.HBM

    factor, *packs = call(
        pack_factor,
        [shape(*factor.shape), strip, strip, own, own],
        [hbm],
        [pltpu.SemaphoreType.DMA((len(CHUNKS),))],
        limit=WIDE_LIMIT,
    )(factor)
    field, to_left, to_right, down, up = call(
        pack_right_side, [plane, strip, strip, own, own], [vmem] * 5, aliases={k: k for k in range(1, 5)}
    )(right_side, *packs)
    right, left = swap(to_left, to_right, "gy", False)
    own_down, own_up = swap(down, up, "gx", True)
    (weighted,) = call(
        weigh,
        [shape(*stiffness.shape)],
        [hbm] * 2,
        [pltpu.VMEM(intact.shape, jnp.int32), pltpu.SemaphoreType.DMA((2,))],
        pl.CostEstimate(flops=stiffness.size, bytes_accessed=8 * stiffness.size, transcendentals=0),
        WIDE_LIMIT,
    )(stiffness, intact)
    down, up = call(pack_corners, [ends_of_strip] * 2, [vmem] * 3)(right, left, weighted)
    edge, side = call(
        unpack_sides,
        [tiles, shape(PLANES, ROWS, LANES)],
        [vmem] * 5,
        cost=pl.CostEstimate(flops=4 * factor.size, bytes_accessed=8 * factor.size, transcendentals=0),
    )(right, left, own_down, own_up, down)
    corner_down, corner_up = swap(down, up, "gx", True)

    corner, g, z, w, to_left, to_right = call(
        first_half, [tiles, plane, plane, plane, small, small], [vmem] * 11, [wide]
    )(factor, edge, side, weighted, field, right, left, own_down, own_up, corner_down, corner_up)
    field_right, field_left = swap(to_left, to_right, "gy", False)
    down, up = call(pack_field, [edges] * 2, [vmem] * 3)(w, field_right, field_left)
    field_down, field_up = swap(down, up, "gx", True)
    u, au, sums = call(second_half, [plane, plane, shape(nx, 1, LANES)], [vmem] * 12, [wide])(
        factor, edge, side, weighted, corner, g, z, w, field_right, field_left, field_down, field_up
    )
    sums = gathered_sum(sums, "gx")
    sums = gathered_sum(jnp.broadcast_to(sums[None], (ny, 1, LANES)), "gy")
    x, r = call(finish, [plane] * 2, [vmem] * 6)(sums, field, z, w, u, au)
    return x, r


def solution(mesh):
    in_specs = (
        P(None, "gx", "gy"),
        P(None, None, None, "gx", "gy"),
        P(None, None, None, "gx", "gy"),
        P(None, "gx", "gy"),
    )
    out_specs = (P(None, "gx", "gy"), P(None, "gx", "gy"))
    return jax.shard_map(local, mesh=mesh, in_specs=in_specs, out_specs=out_specs, check_vma=False)
```

```python
import jax
import jax.numpy as jnp
from jax import lax
from jax.experimental import pallas as pl
from jax.experimental.pallas import tpu as pltpu
from jax.sharding import PartitionSpec as P

NZ = 4
GX = ("chip", "core")
ROWS = 16
LANES = 128
LOWER = 17
PLANES = LOWER * 9
OWN_TILES = (PLANES + 1) // 2 + 2
CENTRE = 0.8
VMEM_LIMIT = 24 * 1024 * 1024
WIDE_LIMIT = 51 * 1024 * 1024
PACK_LIMIT = 52 * 1024 * 1024 - 384 * 1024


def bond_offsets():
    return [
        (a, b, c)
        for a in range(-2, 3)
        for b in range(-2, 3)
        for c in range(-2, 3)
        if a * a + b * b + c * c <= 4
    ]


OFFSETS = bond_offsets()


def iota(rows, axis):
    return lax.broadcasted_iota(jnp.int32, (rows, LANES), axis)


def entry(p):
    return (p // 9, (p // 3) % 3, p % 3)


def seating():
    hosts = [(p, 3 if OFFSETS[p // 9][2] > 0 else 0) for p in range(PLANES) if abs(OFFSETS[p // 9][2]) == 1]
    below = OFFSETS.index((0, 0, -2))
    wanted = [(p, layer) for p in [*range(0, 9), *range(18, 24)] for layer in range(NZ)]
    wanted += [(p, layer) for p in range(9 * below, 9 * below + 9) for layer in (2, 3)]
    riders, seats = {}, {}
    for (guest, layer), (host, free) in zip(wanted, hosts):
        riders[host] = (guest, layer, free)
        seats.setdefault(guest, []).append((host, layer, free))
    return riders, seats


RIDERS, SEATS = seating()
CARRIERS = [p for p in range(PLANES) if p not in SEATS]
GROUPS = (len(CARRIERS) + 7) // 8
assert len(CARRIERS) % 8 == 1 and sum(map(len, SEATS.values())) == len(RIDERS)


def layer_of(rows):
    return iota(rows, 1) & (NZ - 1)


def carried(factor, p):
    plane = factor[entry(p)]
    if p in RIDERS:
        guest, layer, free = RIDERS[p]
        moved = factor[entry(guest)]
        if free != layer:
            moved = pltpu.roll(moved, (free - layer) % LANES, 1)
        plane = jnp.where(layer_of(ROWS) == free, moved, plane)
    return plane


def seat_guests(store):
    rows = store.shape[1]
    for guest, seats in SEATS.items():
        plane = None
        for host, layer, free in seats:
            moved = store[host]
            if free != layer:
                moved = pltpu.roll(moved, (layer - free) % LANES, 1)
            plane = moved if plane is None else jnp.where(layer_of(rows) == layer, moved, plane)
        store[guest] = plane


def pack_lanes(planes, width, first=0):
    shift = width.bit_length() - 1
    slots = LANES // width
    slot = iota(ROWS, 1) >> shift
    halves = [None, None]
    for k, plane in enumerate(planes, first):
        rolled = pltpu.roll(plane, k * width, 1) if k else plane
        held = halves[k & 1]
        if held is not None:
            rolled = jnp.where((slot == k) | (slot == (k - 1) % slots), rolled, held)
        halves[k & 1] = rolled
    even, odd = (jnp.zeros((ROWS, LANES), jnp.float32) if half is None else half for half in halves)
    is_even = (slot & 1) == 0
    return jnp.where(is_even, even, odd), jnp.where(is_even, odd, even)


def unpack_lanes(right, left, width, count, first=0):
    shift = width.bit_length() - 1
    even = ((iota(right.shape[0], 1) >> shift) & 1) == 0
    mixed = (jnp.where(even, right, left), jnp.where(even, left, right))
    return [pltpu.roll(mixed[k & 1], LANES - k * width, 1) if k else mixed[0] for k in range(first, first + count)]


def pack_rows(first, second):
    upper = iota(8, 0) < 4
    down = jnp.where(upper, first[:8], pltpu.roll(second[:8], 4, 0))
    up = jnp.where(upper, pltpu.roll(second[8:], 4, 0), first[8:])
    return down, up


def unpack_rows(down, up):
    upper = iota(8, 0) < 4
    return jnp.where(upper, down, up), pltpu.roll(jnp.where(upper, up, down), 4, 0)


CHUNKS = ((0, 6), (6, 11), (11, LOWER))


def pack_factor(factor_hbm, factor, to_left, to_right, sems):
    copies = []
    for k, (low, high) in enumerate(CHUNKS):
        part = pl.ds(low, high - low)
        copies.append(pltpu.make_async_copy(factor_hbm.at[part], factor.at[part], sems.at[k]))
    for copy in copies:
        copy.start()
    group = 0
    for k, (low, high) in enumerate(CHUNKS):
        copies[k].wait()
        ready = 9 * high
        while group < GROUPS:
            members = CARRIERS[8 * group : 8 * group + 8]
            if max([*members, *(RIDERS[p][0] for p in members if p in RIDERS)]) >= ready:
                break
            to_left[group], to_right[group] = pack_lanes([carried(factor, p) for p in members], 16)
            group += 1


def pack_right_side(field, left_in, right_in, kept, to_left, to_right):
    kept[...] = field[...]
    to_left[...] = left_in[...]
    to_right[...] = right_in[...]
    last, lane = GROUPS - 1, iota(ROWS, 1)
    low, high = pack_lanes([field[k] for k in range(3)], 32, 1)
    to_left[last] = jnp.where(lane < 32, left_in[last], low)
    to_right[last] = jnp.where(lane >= 96, right_in[last], high)


def pack_own(factor, field, down, up):
    for tile in range(OWN_TILES - 2):
        first, second = 2 * tile, min(2 * tile + 1, PLANES - 1)
        down[tile], up[tile] = pack_rows(factor[entry(first)], factor[entry(second)])
    down[OWN_TILES - 2], up[OWN_TILES - 2] = pack_rows(field[0], field[1])
    down[OWN_TILES - 1], up[OWN_TILES - 1] = pack_rows(field[2], field[2])


def weigh(stiffness_hbm, intact_hbm, weighted, intact, sems):
    bonds = pltpu.make_async_copy(intact_hbm, intact, sems.at[0])
    blocks = pltpu.make_async_copy(stiffness_hbm, weighted, sems.at[1])
    bonds.start()
    blocks.start()
    bonds.wait()
    blocks.wait()
    for index, (_, _, dz) in enumerate(OFFSETS):
        if index != 16:
            weight = clipped(intact[index if index < 16 else index - 1].astype(jnp.float32), dz)
            for i in range(3):
                for j in range(3):
                    weighted[index, i, j] = weighted[index, i, j] * weight


def pack_corners(right, left, weighted, down, up):
    for g in range(GROUPS):
        down[g], up[g] = pack_rows(right[g], left[g])


def pack_field(field, right, left, down, up):
    down[0], up[0] = pack_rows(field[0], field[1])
    down[1], up[1] = pack_rows(field[2], field[2])
    down[2], up[2] = pack_rows(right[0], left[0])


def unpack_sides(right, left, own_down, own_up, corner_down, edge, side):
    for m in range(OWN_TILES - 2):
        first, second = unpack_rows(own_down[m], own_up[m])
        edge[2 * m] = first
        if 2 * m + 1 < PLANES:
            edge[2 * m + 1] = second
    for g in range(GROUPS):
        members = CARRIERS[8 * g : 8 * g + 8]
        for p, plane in zip(members, unpack_lanes(right[g], left[g], 16, len(members))):
            side[p] = plane
    seat_guests(side)


def unpack_corners(corner_down, corner_up, corner):
    for g in range(GROUPS):
        right, left = unpack_rows(corner_down[g], corner_up[g])
        members = CARRIERS[8 * g : 8 * g + 8]
        for p, plane in zip(members, unpack_lanes(right, left, 16, len(members))):
            corner[p] = plane
    seat_guests(corner)


def put(wide, component, tile, values):
    column = pl.ds(tile * LANES, LANES)
    wide[component, 0:8, column] = values[16:24]
    wide[component, 8:32, column] = values
    wide[component, 32:40, column] = values[0:8]


def get(wide, component, tile, shift, rows):
    return wide[component, 8 + shift : 8 + shift + rows, tile * LANES : (tile + 1) * LANES]


def shifted(near, far, by):
    if by == 0:
        return near
    lane = iota(near.shape[0], 1)
    kept = lane >= by if by > 0 else lane < LANES + by
    return pltpu.roll(jnp.where(kept, near, far), (-by) % LANES, 1)


def layer_ok(rows, dz):
    z = (iota(rows, 1) & (NZ - 1)) + dz
    return (z >= 0) & (z < NZ)


def clipped(values, dz):
    return values if dz == 0 else jnp.where(layer_ok(values.shape[0], dz), values, 0.0)


def by_dx(offsets):
    found = {}
    for index, (dx, dy, dz) in enumerate(offsets):
        found.setdefault(dx, []).append((index, dy, dz))
    return found


def mask_edge(values, edge_out):
    return jnp.concatenate([values[:16], jnp.where(edge_out, 0.0, values[16:24])], axis=0)


def coefficient(blocks, plane, tile):
    factor, edge, side, corner = blocks
    if tile:
        return jnp.concatenate([side[plane], corner[plane]], axis=0)
    return jnp.concatenate([factor[entry(plane)], edge[plane]], axis=0)


def apply_factor(blocks, wide, edge_out):
    total = [[jnp.zeros((24, LANES), jnp.float32) for _ in range(2)] for _ in range(3)]
    for dx, members in by_dx(OFFSETS[:LOWER]).items():
        base = [[get(wide, j, t, dx, 24) for t in range(2)] for j in range(3)]
        for index, dy, dz in members:
            by = dy * NZ + dz
            for j in range(3):
                for t in range(2):
                    piece = clipped(shifted(base[j][t], base[j][1 - t], by), dz)
                    for i in range(3):
                        total[i][t] += coefficient(blocks, 9 * index + 3 * i + j, t) * piece
    return [[mask_edge(total[i][t], edge_out) for t in range(2)] for i in range(3)]


def apply_transpose(blocks, image, wide, edge_out, side_out):
    clips = {dz: [[clipped(image[j][t], dz) for t in range(2)] for j in range(3)] for dz in range(-2, 2)}
    final = [[jnp.zeros((24, LANES), jnp.float32) for _ in range(2)] for _ in range(3)]
    for dx, members in sorted(by_dx(OFFSETS[:LOWER]).items()):
        total = [[jnp.zeros((24, LANES), jnp.float32) for _ in range(2)] for _ in range(3)]
        for index, dy, dz in members:
            by = -(dy * NZ + dz)
            for i in range(3):
                parts = []
                for t in range(2):
                    part = coefficient(blocks, 9 * index + i, t) * clips[dz][0][t]
                    for j in range(1, 3):
                        part += coefficient(blocks, 9 * index + 3 * j + i, t) * clips[dz][j][t]
                    parts.append(part)
                for t in range(2):
                    total[i][t] += shifted(parts[t], parts[1 - t], by)
        if dx:
            for i in range(3):
                for t in range(2):
                    put(wide, i, t, total[i][t])
            total = [[get(wide, i, t, -dx, 24) for t in range(2)] for i in range(3)]
        final = [[final[i][t] + total[i][t] for t in range(2)] for i in range(3)]
    out = []
    for i in range(3):
        row = []
        for t in range(2):
            values = mask_edge(final[i][t], edge_out)
            row.append(jnp.where(side_out, 0.0, values) if t else values)
        out.append(row)
    return out


def apply_operator(weighted, wide):
    total = [jnp.zeros((ROWS, LANES), jnp.float32) for _ in range(3)]
    for dx, members in by_dx(OFFSETS).items():
        base = [[get(wide, j, t, dx, ROWS) for t in range(2)] for j in range(3)]
        for index, dy, dz in members:
            for j in range(3):
                piece = shifted(base[j][0], base[j][1], dy * NZ + dz)
                for i in range(3):
                    total[i] += weighted[index, i, j] * piece
    return total


def outside():
    ends = []
    for axis in (GX, "gy"):
        place = lax.axis_index(axis)
        ends += [(place == 0).astype(jnp.int32), (place == lax.axis_size(axis) - 1).astype(jnp.int32)]
    sub = iota(8, 0)
    edge_out = ((sub < 4) & (ends[1] == 1)) | ((sub >= 4) & (ends[0] == 1))
    lane = iota(24, 1)
    side_out = ((lane < LANES // 2) & (ends[3] == 1)) | ((lane >= LANES // 2) & (ends[2] == 1))
    return edge_out, side_out


def chain(blocks, weighted, field, pieces, wide):
    edge_out, side_out = outside()
    (down_a, up_a), (down_b, up_b), (down_c, up_c), right, left = pieces
    edges = [*unpack_rows(down_a, up_a), unpack_rows(down_b, up_b)[0]]
    edge_right, edge_left = unpack_rows(down_c, up_c)
    sides = unpack_lanes(
        jnp.concatenate([right, edge_right], axis=0), jnp.concatenate([left, edge_left], axis=0), 32, 3, 1
    )
    for j in range(3):
        put(wide, j, 0, mask_edge(jnp.concatenate([field[j], edges[j]], axis=0), edge_out))
        put(wide, j, 1, mask_edge(sides[j], edge_out))
    image = apply_factor(blocks, wide, edge_out)
    zvec = apply_transpose(blocks, image, wide, edge_out, side_out)
    for i in range(3):
        for t in range(2):
            put(wide, i, t, zvec[i][t])
    product = apply_operator(weighted, wide)
    return [image[i][0][:ROWS] for i in range(3)], [zvec[i][0][:ROWS] for i in range(3)], product


def first_half(
    factor, edge, side, weighted, field, right, left, own_down, own_up, corner_down, corner_up,
    corner, g_out, z_out, w_out, to_left, to_right, wide,
):
    unpack_corners(corner_down, corner_up, corner)
    a, b, c = OWN_TILES - 2, OWN_TILES - 1, GROUPS - 1
    pieces = (
        (own_down[a], own_up[a]), (own_down[b], own_up[b]), (corner_down[c], corner_up[c]), right[c], left[c],
    )
    image, zvec, product = chain((factor, edge, side, corner), weighted, field, pieces, wide)
    for i in range(3):
        g_out[i], z_out[i], w_out[i] = image[i], zvec[i], product[i]
    to_left[0], to_right[0] = pack_lanes(product, 32, 1)


def dot(first, second):
    whole = first[0] * second[0] + first[1] * second[1] + first[2] * second[2]
    return whole[:8] + whole[8:]


def second_half(
    factor, edge, side, weighted, corner, g_in, z_in, w_in, field_right, field_left, field_down, field_up,
    u_out, au_out, sums, wide,
):
    pieces = tuple((field_down[k], field_up[k]) for k in range(3)) + (field_right[0], field_left[0])
    v, u, au = chain((factor, edge, side, corner), weighted, w_in, pieces, wide)
    for i in range(3):
        u_out[i], au_out[i] = u[i], au[i]
    g, z, w = ([ref[i] for i in range(3)] for ref in (g_in, z_in, w_in))
    g1 = [g[i] - CENTRE * v[i] for i in range(3)]
    z1 = [z[i] - CENTRE * u[i] for i in range(3)]
    az1 = [w[i] - CENTRE * au[i] for i in range(3)]
    parts = [
        dot(g, g), dot(z, w), dot(g1, g1), dot(g1, v), dot(v, v), dot(z1, az1),
        dot(u, az1) + dot(z1, au), dot(u, au), dot(z1, w) + dot(z, az1), dot(u, w) + dot(z, au),
    ]
    lane = lax.broadcasted_iota(jnp.int32, (1, LANES), 1)
    row = jnp.zeros((1, LANES), jnp.float32)
    for k, part in enumerate(parts):
        value = jnp.sum(jnp.sum(part, axis=0, keepdims=True), axis=1, keepdims=True)
        row = jnp.where(lane == k, value, row)
    for k in range(sums.shape[0]):
        sums[k] = row


def finish(sums, field, z_in, w_in, u_in, au_in, x_out, r_out):
    row = sums[...]
    lane = lax.broadcasted_iota(jnp.int32, (1, LANES), 1)
    s = [jnp.sum(jnp.where(lane == k, row, 0.0), axis=1, keepdims=True) for k in range(10)]
    alpha = s[0] / s[1]
    off = alpha - CENTRE
    rho = s[2] - 2.0 * off * s[3] + off * off * s[4]
    beta = rho / s[0]
    zaz = s[5] - off * s[6] + off * off * s[7]
    cross = s[8] - off * s[9]
    last = rho / (zaz + beta * cross + beta * beta * s[1])
    kept = alpha + last * (1.0 + beta)
    turned = last * alpha
    for i in range(3):
        x_out[i] = kept * z_in[i] - turned * u_in[i]
        r_out[i] = field[i] - (kept * w_in[i] - turned * au_in[i])


def shape(*dims):
    return jax.ShapeDtypeStruct(dims, jnp.float32)


def call(body, outs, spaces, scratch=(), cost=None, limit=VMEM_LIMIT, aliases=None):
    return pl.pallas_call(
        body,
        out_shape=outs,
        in_specs=[pl.BlockSpec(memory_space=space) for space in spaces],
        out_specs=[pl.BlockSpec(memory_space=pltpu.VMEM)] * len(outs),
        scratch_shapes=list(scratch),
        compiler_params=pltpu.CompilerParams(vmem_limit_bytes=limit),
        cost_estimate=cost,
        input_output_aliases=aliases or {},
        name=body.__name__,
    )


def swap(first, second, axis, wrap):
    count = lax.axis_size(axis)
    ends = count if wrap else count - 1
    back = [((i + 1) % count, i) for i in range(ends)]
    ahead = [(i, (i + 1) % count) for i in range(ends)]
    return lax.ppermute(first, axis, back), lax.ppermute(second, axis, ahead)


def gathered_sum(rows, axis):
    return jnp.sum(lax.all_to_all(rows, axis, 0, 0), axis=0)


def local(right_side, stiffness, factor, intact):
    nx, ny = lax.axis_size(GX), lax.axis_size("gy")
    plane = shape(3, ROWS, LANES)
    strip = shape(GROUPS, ROWS, LANES)
    own = shape(OWN_TILES, 8, LANES)
    ends_of_strip = shape(GROUPS, 8, LANES)
    small = shape(1, ROWS, LANES)
    edges = shape(3, 8, LANES)
    tiles = shape(PLANES, 8, LANES)
    wide = pltpu.VMEM((3, 40, 2 * LANES), jnp.float32)
    vmem, hbm = pltpu.VMEM, pltpu.HBM

    factor, *packs = call(
        pack_factor,
        [shape(*factor.shape), strip, strip],
        [hbm],
        [pltpu.SemaphoreType.DMA((len(CHUNKS),))],
        limit=PACK_LIMIT,
    )(factor)
    field, to_left, to_right = call(
        pack_right_side, [plane, strip, strip], [vmem] * 3, aliases={1: 1, 2: 2}
    )(right_side, *packs)
    right, left = swap(to_left, to_right, "gy", False)
    down, up = call(
        pack_own,
        [own] * 2,
        [vmem] * 2,
        cost=pl.CostEstimate(flops=4 * factor.size, bytes_accessed=8 * factor.size, transcendentals=0),
    )(factor, field)
    own_down, own_up = swap(down, up, GX, True)
    (weighted,) = call(
        weigh,
        [shape(*stiffness.shape)],
        [hbm] * 2,
        [pltpu.VMEM(intact.shape, jnp.int32), pltpu.SemaphoreType.DMA((2,))],
        pl.CostEstimate(flops=stiffness.size, bytes_accessed=8 * stiffness.size, transcendentals=0),
        WIDE_LIMIT,
    )(stiffness, intact)
    down, up = call(pack_corners, [ends_of_strip] * 2, [vmem] * 3)(right, left, weighted)
    edge, side = call(
        unpack_sides,
        [tiles, shape(PLANES, ROWS, LANES)],
        [vmem] * 5,
        cost=pl.CostEstimate(flops=4 * factor.size, bytes_accessed=8 * factor.size, transcendentals=0),
    )(right, left, own_down, own_up, down)
    corner_down, corner_up = swap(down, up, GX, True)

    corner, g, z, w, to_left, to_right = call(
        first_half, [tiles, plane, plane, plane, small, small], [vmem] * 11, [wide]
    )(factor, edge, side, weighted, field, right, left, own_down, own_up, corner_down, corner_up)
    field_right, field_left = swap(to_left, to_right, "gy", False)
    down, up = call(pack_field, [edges] * 2, [vmem] * 3)(w, field_right, field_left)
    field_down, field_up = swap(down, up, GX, True)
    u, au, sums = call(second_half, [plane, plane, shape(2 * ny, 1, LANES)], [vmem] * 12, [wide])(
        factor, edge, side, weighted, corner, g, z, w, field_right, field_left, field_down, field_up
    )
    sums = gathered_sum(sums, ("core", "gy"))
    sums = gathered_sum(jnp.broadcast_to(sums[None], (nx // 2, 1, LANES)), "chip")
    x, r = call(finish, [plane] * 2, [vmem] * 6)(sums, field, z, w, u, au)
    return x, r


def solution(mesh):
    nx, ny = mesh.devices.shape
    mesh = jax.sharding.Mesh(mesh.devices.reshape(nx // 2, 2, ny), ("chip", "core", "gy"))
    in_specs = (
        P(None, GX, "gy"),
        P(None, None, None, GX, "gy"),
        P(None, None, None, GX, "gy"),
        P(None, GX, "gy"),
    )
    out_specs = (P(None, GX, "gy"), P(None, GX, "gy"))
    return jax.shard_map(local, mesh=mesh, in_specs=in_specs, out_specs=out_specs, check_vma=False)
```

```python
import jax
import jax.numpy as jnp
from jax import lax
from jax.experimental import pallas as pl
from jax.experimental.pallas import tpu as pltpu
from jax.sharding import PartitionSpec as P

NZ = 4
GX = ("chip", "core")
ROWS = 16
LANES = 128
LOWER = 17
PLANES = LOWER * 9
OWN_TILES = (PLANES + 1) // 2 + 2
CENTRE = 0.8
VMEM_LIMIT = 24 * 1024 * 1024
WIDE_LIMIT = 51 * 1024 * 1024
PACK_LIMIT = 52 * 1024 * 1024 - 384 * 1024


def bond_offsets():
    return [
        (a, b, c)
        for a in range(-2, 3)
        for b in range(-2, 3)
        for c in range(-2, 3)
        if a * a + b * b + c * c <= 4
    ]


OFFSETS = bond_offsets()


def iota(rows, axis):
    return lax.broadcasted_iota(jnp.int32, (rows, LANES), axis)


def entry(p):
    return (p // 9, (p // 3) % 3, p % 3)


def seating():
    hosts = [(p, 3 if OFFSETS[p // 9][2] > 0 else 0) for p in range(PLANES) if abs(OFFSETS[p // 9][2]) == 1]
    below = OFFSETS.index((0, 0, -2))
    wanted = [(p, layer) for p in [*range(0, 9), *range(18, 24)] for layer in range(NZ)]
    wanted += [(p, layer) for p in range(9 * below, 9 * below + 9) for layer in (2, 3)]
    riders, seats = {}, {}
    for (guest, layer), (host, free) in zip(wanted, hosts):
        riders[host] = (guest, layer, free)
        seats.setdefault(guest, []).append((host, layer, free))
    return riders, seats


RIDERS, SEATS = seating()
CARRIERS = [p for p in range(PLANES) if p not in SEATS]
GROUPS = (len(CARRIERS) + 7) // 8
assert len(CARRIERS) % 8 == 1 and sum(map(len, SEATS.values())) == len(RIDERS)


def layer_of(rows):
    return iota(rows, 1) & (NZ - 1)


def carried(factor, p):
    plane = factor[entry(p)]
    if p in RIDERS:
        guest, layer, free = RIDERS[p]
        moved = factor[entry(guest)]
        if free != layer:
            moved = pltpu.roll(moved, (free - layer) % LANES, 1)
        plane = jnp.where(layer_of(ROWS) == free, moved, plane)
    return plane


def seat_guests(store):
    rows = store.shape[1]
    for guest, seats in SEATS.items():
        plane = None
        for host, layer, free in seats:
            moved = store[host]
            if free != layer:
                moved = pltpu.roll(moved, (layer - free) % LANES, 1)
            plane = moved if plane is None else jnp.where(layer_of(rows) == layer, moved, plane)
        store[guest] = plane


def pack_lanes(planes, width, first=0):
    shift = width.bit_length() - 1
    slots = LANES // width
    slot = iota(ROWS, 1) >> shift
    halves = [None, None]
    for k, plane in enumerate(planes, first):
        rolled = pltpu.roll(plane, k * width, 1) if k else plane
        held = halves[k & 1]
        if held is not None:
            rolled = jnp.where((slot == k) | (slot == (k - 1) % slots), rolled, held)
        halves[k & 1] = rolled
    even, odd = (jnp.zeros((ROWS, LANES), jnp.float32) if half is None else half for half in halves)
    is_even = (slot & 1) == 0
    return jnp.where(is_even, even, odd), jnp.where(is_even, odd, even)


def unpack_lanes(right, left, width, count, first=0):
    shift = width.bit_length() - 1
    even = ((iota(right.shape[0], 1) >> shift) & 1) == 0
    mixed = (jnp.where(even, right, left), jnp.where(even, left, right))
    return [pltpu.roll(mixed[k & 1], LANES - k * width, 1) if k else mixed[0] for k in range(first, first + count)]


def pack_rows(first, second):
    upper = iota(8, 0) < 4
    down = jnp.where(upper, first[:8], pltpu.roll(second[:8], 4, 0))
    up = jnp.where(upper, pltpu.roll(second[8:], 4, 0), first[8:])
    return down, up


def unpack_rows(down, up):
    upper = iota(8, 0) < 4
    return jnp.where(upper, down, up), pltpu.roll(jnp.where(upper, up, down), 4, 0)


CHUNKS = ((0, 8), (8, 13), (13, LOWER))


def pack_factor(factor_hbm, factor, to_left, to_right, sems):
    copies = []
    for k, (low, high) in enumerate(CHUNKS):
        part = pl.ds(low, high - low)
        copies.append(pltpu.make_async_copy(factor_hbm.at[part], factor.at[part], sems.at[k]))
    for copy in copies:
        copy.start()
    group = 0
    for k, (low, high) in enumerate(CHUNKS):
        copies[k].wait()
        ready = 9 * high
        while group < GROUPS:
            members = CARRIERS[8 * group : 8 * group + 8]
            if max([*members, *(RIDERS[p][0] for p in members if p in RIDERS)]) >= ready:
                break
            to_left[group], to_right[group] = pack_lanes([carried(factor, p) for p in members], 16)
            group += 1


def pack_right_side(field, left_in, right_in, kept, to_left, to_right):
    kept[...] = field[...]
    to_left[...] = left_in[...]
    to_right[...] = right_in[...]
    last, lane = GROUPS - 1, iota(ROWS, 1)
    low, high = pack_lanes([field[k] for k in range(3)], 32, 1)
    to_left[last] = jnp.where(lane < 32, left_in[last], low)
    to_right[last] = jnp.where(lane >= 96, right_in[last], high)


def pack_own(factor, field, down, up):
    for tile in range(OWN_TILES - 2):
        first, second = 2 * tile, min(2 * tile + 1, PLANES - 1)
        down[tile], up[tile] = pack_rows(factor[entry(first)], factor[entry(second)])
    down[OWN_TILES - 2], up[OWN_TILES - 2] = pack_rows(field[0], field[1])
    down[OWN_TILES - 1], up[OWN_TILES - 1] = pack_rows(field[2], field[2])


def weigh(stiffness_hbm, intact_hbm, weighted, intact, sems):
    bonds = pltpu.make_async_copy(intact_hbm, intact, sems.at[0])
    blocks = pltpu.make_async_copy(stiffness_hbm, weighted, sems.at[1])
    bonds.start()
    blocks.start()
    bonds.wait()
    blocks.wait()
    for index, (_, _, dz) in enumerate(OFFSETS):
        if index != 16:
            weight = clipped(intact[index if index < 16 else index - 1].astype(jnp.float32), dz)
            for i in range(3):
                for j in range(3):
                    weighted[index, i, j] = weighted[index, i, j] * weight


def pack_corners(right, left, weighted, down, up):
    for g in range(GROUPS):
        down[g], up[g] = pack_rows(right[g], left[g])


def pack_field(field, right, left, down, up):
    down[0], up[0] = pack_rows(field[0], field[1])
    down[1], up[1] = pack_rows(field[2], field[2])
    down[2], up[2] = pack_rows(right[0], left[0])


def unpack_sides(right, left, own_down, own_up, corner_down, edge, side):
    for m in range(OWN_TILES - 2):
        first, second = unpack_rows(own_down[m], own_up[m])
        edge[2 * m] = first
        if 2 * m + 1 < PLANES:
            edge[2 * m + 1] = second
    for g in range(GROUPS):
        members = CARRIERS[8 * g : 8 * g + 8]
        for p, plane in zip(members, unpack_lanes(right[g], left[g], 16, len(members))):
            side[p] = plane
    seat_guests(side)


def unpack_corners(corner_down, corner_up, corner):
    for g in range(GROUPS):
        right, left = unpack_rows(corner_down[g], corner_up[g])
        members = CARRIERS[8 * g : 8 * g + 8]
        for p, plane in zip(members, unpack_lanes(right, left, 16, len(members))):
            corner[p] = plane
    seat_guests(corner)


def put(wide, component, tile, values):
    column = pl.ds(tile * LANES, LANES)
    wide[component, 0:8, column] = values[16:24]
    wide[component, 8:32, column] = values
    wide[component, 32:40, column] = values[0:8]


def get(wide, component, tile, shift, rows):
    return wide[component, 8 + shift : 8 + shift + rows, tile * LANES : (tile + 1) * LANES]


def shifted(near, far, by):
    if by == 0:
        return near
    lane = iota(near.shape[0], 1)
    kept = lane >= by if by > 0 else lane < LANES + by
    return pltpu.roll(jnp.where(kept, near, far), (-by) % LANES, 1)


def layer_ok(rows, dz):
    z = (iota(rows, 1) & (NZ - 1)) + dz
    return (z >= 0) & (z < NZ)


def clipped(values, dz):
    return values if dz == 0 else jnp.where(layer_ok(values.shape[0], dz), values, 0.0)


def by_dx(offsets):
    found = {}
    for index, (dx, dy, dz) in enumerate(offsets):
        found.setdefault(dx, []).append((index, dy, dz))
    return found


def mask_edge(values, edge_out):
    return jnp.concatenate([values[:16], jnp.where(edge_out, 0.0, values[16:24])], axis=0)


def coefficient(blocks, plane, tile):
    factor, edge, side, corner = blocks
    if tile:
        return jnp.concatenate([side[plane], corner[plane]], axis=0)
    return jnp.concatenate([factor[entry(plane)], edge[plane]], axis=0)


def apply_factor(blocks, wide, edge_out):
    total = [[jnp.zeros((24, LANES), jnp.float32) for _ in range(2)] for _ in range(3)]
    for dx, members in by_dx(OFFSETS[:LOWER]).items():
        base = [[get(wide, j, t, dx, 24) for t in range(2)] for j in range(3)]
        for index, dy, dz in members:
            by = dy * NZ + dz
            for j in range(3):
                for t in range(2):
                    piece = clipped(shifted(base[j][t], base[j][1 - t], by), dz)
                    for i in range(3):
                        total[i][t] += coefficient(blocks, 9 * index + 3 * i + j, t) * piece
    return [[mask_edge(total[i][t], edge_out) for t in range(2)] for i in range(3)]


def apply_transpose(blocks, image, wide, edge_out, side_out):
    clips = {dz: [[clipped(image[j][t], dz) for t in range(2)] for j in range(3)] for dz in range(-2, 2)}
    final = [[jnp.zeros((24, LANES), jnp.float32) for _ in range(2)] for _ in range(3)]
    for dx, members in sorted(by_dx(OFFSETS[:LOWER]).items()):
        total = [[jnp.zeros((24, LANES), jnp.float32) for _ in range(2)] for _ in range(3)]
        for index, dy, dz in members:
            by = -(dy * NZ + dz)
            for i in range(3):
                parts = []
                for t in range(2):
                    part = coefficient(blocks, 9 * index + i, t) * clips[dz][0][t]
                    for j in range(1, 3):
                        part += coefficient(blocks, 9 * index + 3 * j + i, t) * clips[dz][j][t]
                    parts.append(part)
                for t in range(2):
                    total[i][t] += shifted(parts[t], parts[1 - t], by)
        if dx:
            for i in range(3):
                for t in range(2):
                    put(wide, i, t, total[i][t])
            total = [[get(wide, i, t, -dx, 24) for t in range(2)] for i in range(3)]
        final = [[final[i][t] + total[i][t] for t in range(2)] for i in range(3)]
    out = []
    for i in range(3):
        row = []
        for t in range(2):
            values = mask_edge(final[i][t], edge_out)
            row.append(jnp.where(side_out, 0.0, values) if t else values)
        out.append(row)
    return out


def apply_operator(weighted, wide):
    total = [jnp.zeros((ROWS, LANES), jnp.float32) for _ in range(3)]
    for dx, members in by_dx(OFFSETS).items():
        base = [[get(wide, j, t, dx, ROWS) for t in range(2)] for j in range(3)]
        for index, dy, dz in members:
            for j in range(3):
                piece = shifted(base[j][0], base[j][1], dy * NZ + dz)
                for i in range(3):
                    total[i] += weighted[index, i, j] * piece
    return total


def outside():
    ends = []
    for axis in (GX, "gy"):
        place = lax.axis_index(axis)
        ends += [(place == 0).astype(jnp.int32), (place == lax.axis_size(axis) - 1).astype(jnp.int32)]
    sub = iota(8, 0)
    edge_out = ((sub < 4) & (ends[1] == 1)) | ((sub >= 4) & (ends[0] == 1))
    lane = iota(24, 1)
    side_out = ((lane < LANES // 2) & (ends[3] == 1)) | ((lane >= LANES // 2) & (ends[2] == 1))
    return edge_out, side_out


def chain(blocks, weighted, field, pieces, wide):
    edge_out, side_out = outside()
    (down_a, up_a), (down_b, up_b), (down_c, up_c), right, left = pieces
    edges = [*unpack_rows(down_a, up_a), unpack_rows(down_b, up_b)[0]]
    edge_right, edge_left = unpack_rows(down_c, up_c)
    sides = unpack_lanes(
        jnp.concatenate([right, edge_right], axis=0), jnp.concatenate([left, edge_left], axis=0), 32, 3, 1
    )
    for j in range(3):
        put(wide, j, 0, mask_edge(jnp.concatenate([field[j], edges[j]], axis=0), edge_out))
        put(wide, j, 1, mask_edge(sides[j], edge_out))
    image = apply_factor(blocks, wide, edge_out)
    zvec = apply_transpose(blocks, image, wide, edge_out, side_out)
    for i in range(3):
        for t in range(2):
            put(wide, i, t, zvec[i][t])
    product = apply_operator(weighted, wide)
    return [image[i][0][:ROWS] for i in range(3)], [zvec[i][0][:ROWS] for i in range(3)], product


def first_half(
    factor, edge, side, weighted, field, right, left, own_down, own_up, corner_down, corner_up,
    corner, g_out, z_out, w_out, to_left, to_right, wide,
):
    unpack_corners(corner_down, corner_up, corner)
    a, b, c = OWN_TILES - 2, OWN_TILES - 1, GROUPS - 1
    pieces = (
        (own_down[a], own_up[a]), (own_down[b], own_up[b]), (corner_down[c], corner_up[c]), right[c], left[c],
    )
    image, zvec, product = chain((factor, edge, side, corner), weighted, field, pieces, wide)
    for i in range(3):
        g_out[i], z_out[i], w_out[i] = image[i], zvec[i], product[i]
    to_left[0], to_right[0] = pack_lanes(product, 32, 1)


def dot(first, second):
    whole = first[0] * second[0] + first[1] * second[1] + first[2] * second[2]
    return whole[:8] + whole[8:]


def second_half(
    factor, edge, side, weighted, corner, g_in, z_in, w_in, field_right, field_left, field_down, field_up,
    u_out, au_out, sums, wide,
):
    pieces = tuple((field_down[k], field_up[k]) for k in range(3)) + (field_right[0], field_left[0])
    v, u, au = chain((factor, edge, side, corner), weighted, w_in, pieces, wide)
    for i in range(3):
        u_out[i], au_out[i] = u[i], au[i]
    g, z, w = ([ref[i] for i in range(3)] for ref in (g_in, z_in, w_in))
    g1 = [g[i] - CENTRE * v[i] for i in range(3)]
    z1 = [z[i] - CENTRE * u[i] for i in range(3)]
    az1 = [w[i] - CENTRE * au[i] for i in range(3)]
    parts = [
        dot(g, g), dot(z, w), dot(g1, g1), dot(g1, v), dot(v, v), dot(z1, az1),
        dot(u, az1) + dot(z1, au), dot(u, au), dot(z1, w) + dot(z, az1), dot(u, w) + dot(z, au),
    ]
    lane = lax.broadcasted_iota(jnp.int32, (1, LANES), 1)
    row = jnp.zeros((1, LANES), jnp.float32)
    for k, part in enumerate(parts):
        value = jnp.sum(jnp.sum(part, axis=0, keepdims=True), axis=1, keepdims=True)
        row = jnp.where(lane == k, value, row)
    for k in range(sums.shape[0]):
        sums[k] = row


def finish(sums, field, z_in, w_in, u_in, au_in, x_out, r_out):
    row = sums[...]
    lane = lax.broadcasted_iota(jnp.int32, (1, LANES), 1)
    s = [jnp.sum(jnp.where(lane == k, row, 0.0), axis=1, keepdims=True) for k in range(10)]
    alpha = s[0] / s[1]
    off = alpha - CENTRE
    rho = s[2] - 2.0 * off * s[3] + off * off * s[4]
    beta = rho / s[0]
    zaz = s[5] - off * s[6] + off * off * s[7]
    cross = s[8] - off * s[9]
    last = rho / (zaz + beta * cross + beta * beta * s[1])
    kept = alpha + last * (1.0 + beta)
    turned = last * alpha
    for i in range(3):
        x_out[i] = kept * z_in[i] - turned * u_in[i]
        r_out[i] = field[i] - (kept * w_in[i] - turned * au_in[i])


def shape(*dims):
    return jax.ShapeDtypeStruct(dims, jnp.float32)


def call(body, outs, spaces, scratch=(), cost=None, limit=VMEM_LIMIT, aliases=None):
    return pl.pallas_call(
        body,
        out_shape=outs,
        in_specs=[pl.BlockSpec(memory_space=space) for space in spaces],
        out_specs=[pl.BlockSpec(memory_space=pltpu.VMEM)] * len(outs),
        scratch_shapes=list(scratch),
        compiler_params=pltpu.CompilerParams(vmem_limit_bytes=limit),
        cost_estimate=cost,
        input_output_aliases=aliases or {},
        name=body.__name__,
    )


def swap(first, second, axis, wrap):
    count = lax.axis_size(axis)
    ends = count if wrap else count - 1
    back = [((i + 1) % count, i) for i in range(ends)]
    ahead = [(i, (i + 1) % count) for i in range(ends)]
    return lax.ppermute(first, axis, back), lax.ppermute(second, axis, ahead)


def gathered_sum(rows, axis):
    return jnp.sum(lax.all_to_all(rows, axis, 0, 0), axis=0)


def local(right_side, stiffness, factor, intact):
    nx, ny = lax.axis_size(GX), lax.axis_size("gy")
    plane = shape(3, ROWS, LANES)
    strip = shape(GROUPS, ROWS, LANES)
    own = shape(OWN_TILES, 8, LANES)
    ends_of_strip = shape(GROUPS, 8, LANES)
    small = shape(1, ROWS, LANES)
    edges = shape(3, 8, LANES)
    tiles = shape(PLANES, 8, LANES)
    wide = pltpu.VMEM((3, 40, 2 * LANES), jnp.float32)
    vmem, hbm = pltpu.VMEM, pltpu.HBM

    factor, *packs = call(
        pack_factor,
        [shape(*factor.shape), strip, strip],
        [hbm],
        [pltpu.SemaphoreType.DMA((len(CHUNKS),))],
        limit=PACK_LIMIT,
    )(factor)
    field, to_left, to_right = call(
        pack_right_side, [plane, strip, strip], [vmem] * 3, aliases={1: 1, 2: 2}
    )(right_side, *packs)
    right, left = swap(to_left, to_right, "gy", False)
    down, up = call(
        pack_own,
        [own] * 2,
        [vmem] * 2,
        cost=pl.CostEstimate(flops=4 * factor.size, bytes_accessed=8 * factor.size, transcendentals=0),
    )(factor, field)
    own_down, own_up = swap(down, up, GX, True)
    (weighted,) = call(
        weigh,
        [shape(*stiffness.shape)],
        [hbm] * 2,
        [pltpu.VMEM(intact.shape, jnp.int32), pltpu.SemaphoreType.DMA((2,))],
        pl.CostEstimate(flops=stiffness.size, bytes_accessed=8 * stiffness.size, transcendentals=0),
        WIDE_LIMIT,
    )(stiffness, intact)
    down, up = call(pack_corners, [ends_of_strip] * 2, [vmem] * 3)(right, left, weighted)
    edge, side = call(
        unpack_sides,
        [tiles, shape(PLANES, ROWS, LANES)],
        [vmem] * 5,
        cost=pl.CostEstimate(flops=4 * factor.size, bytes_accessed=8 * factor.size, transcendentals=0),
    )(right, left, own_down, own_up, down)
    corner_down, corner_up = swap(down, up, GX, True)

    corner, g, z, w, to_left, to_right = call(
        first_half, [tiles, plane, plane, plane, small, small], [vmem] * 11, [wide]
    )(factor, edge, side, weighted, field, right, left, own_down, own_up, corner_down, corner_up)
    field_right, field_left = swap(to_left, to_right, "gy", False)
    down, up = call(pack_field, [edges] * 2, [vmem] * 3)(w, field_right, field_left)
    field_down, field_up = swap(down, up, GX, True)
    u, au, sums = call(second_half, [plane, plane, shape(2 * ny, 1, LANES)], [vmem] * 12, [wide])(
        factor, edge, side, weighted, corner, g, z, w, field_right, field_left, field_down, field_up
    )
    sums = gathered_sum(sums, ("core", "gy"))
    sums = gathered_sum(jnp.broadcast_to(sums[None], (nx // 2, 1, LANES)), "chip")
    x, r = call(finish, [plane] * 2, [vmem] * 6)(sums, field, z, w, u, au)
    return x, r


def solution(mesh):
    nx, ny = mesh.devices.shape
    mesh = jax.sharding.Mesh(mesh.devices.reshape(nx // 2, 2, ny), ("chip", "core", "gy"))
    in_specs = (
        P(None, GX, "gy"),
        P(None, None, None, GX, "gy"),
        P(None, None, None, GX, "gy"),
        P(None, GX, "gy"),
    )
    out_specs = (P(None, GX, "gy"), P(None, GX, "gy"))
    return jax.shard_map(local, mesh=mesh, in_specs=in_specs, out_specs=out_specs, check_vma=False)
```
